32 devices in a mesh: tmpl: 32 (over z, y, x, core), dom: 1.
Axes of the slice: x: 2, y: 2, z: 4, core: 2. Of those that a mesh axis runs over, the one named last changes fastest.
Arguments:
- particles: bfloat16 [4096, 16384], P('tmpl', 'dom'), may hold values from -8 to 8
- templates: bfloat16 [128, 18, 16384], P('tmpl', None, 'dom')
- classes: int32 [4096, 1], P('tmpl'), may hold values from 0 to 127; in each aligned block of 128 rows (0 to 127, 128 to 255, ...) at most 2 rows name the same one
- rotations: int32 [4096], P('tmpl'), may hold values from 0 to 17
Outputs:
- class_means: float32 [128, 18, 16384], P('tmpl', None, 'dom')
- weights: bfloat16 [4096], P('tmpl')
The draws below stay inside these ranges and needn't reach their ends.
Inputs may be any that keep to these rules, and one draw needn't show every extreme that they name: `classes`: among the 128 particles of one index of tmpl (aligned blocks of rows) no class appears more than 2 times, and some class appears exactly 2 times.
All inputs are finite; a program needn't handle non-finite values.
Results may differ from the reference program's by a relative error of at most 0.0022.
Values may be sent and summed in bfloat16 or wider, within the bound.
A program may use at most 256 MiB of HBM per device.

```python
import math
import jax
import jax.numpy as jnp
import numpy as np
from jax import lax

CLASSES = 128
ROTATIONS = 18
PIXELS = 16384
PART_DEV = 128
CAPACITY = 2
PARTICLES = 4096
N_TMPL = 32


def template_fields(key):
    base_key = jax.random.fold_in(key, 11)
    noise_key, scale_key = jax.random.split(base_key, 2)
    array_shape = (CLASSES, ROTATIONS, PIXELS)
    noise_field = jax.random.normal(noise_key, array_shape, jnp.float32)
    scales = jnp.exp(jax.random.uniform(scale_key, (CLASSES, ROTATIONS, 1), jnp.float32, 0.0, math.log(10.0)))
    return (noise_field, scales)


def draw_templates(key, part):
    noise_field, scales = template_fields(key)
    return (noise_field * scales / math.sqrt(PIXELS)).astype(jnp.bfloat16)


def draw_particles(key, part):
    noise_field, scales = template_fields(key)
    own_key = jax.random.fold_in(key, 23)
    base_key, source_key, strength_key = jax.random.split(own_key, 3)
    array_shape = (PARTICLES, PIXELS)
    background = jax.random.normal(base_key, array_shape, jnp.float32)
    columns = CLASSES * ROTATIONS
    source = jax.random.randint(source_key, (PARTICLES,), 0, columns)
    strength = jax.random.uniform(strength_key, (PARTICLES,), jnp.float32, 0.7, 2.0)
    flat_fields = noise_field.reshape(columns, PIXELS)
    flat_scales = scales.reshape(columns)
    factor = columns * 21.5 / PIXELS
    amplitude = jnp.minimum(jnp.sqrt(factor * strength) / flat_scales[source], 3.0)
    signal = flat_fields[source] * amplitude[:, None]
    return jnp.clip(background + signal, -8.0, 8.0).astype(jnp.bfloat16)


def place_ends(array, stream_key, least, top_value):
    shape = array.shape
    index_at = [jax.random.randint(jax.random.fold_in(stream_key, axis), (), 0, shape[axis]) for axis in range(len(shape))]
    array = array.at[tuple(index_at)].set(least)
    longest = shape.index(max(shape))
    index_at[longest] = (index_at[longest] + 1) % shape[longest]
    return array.at[tuple(index_at)].set(top_value)


def routed_block(key, own, number, rows, amount, top, limit, slope):
    ranking = jax.random.permutation(key, amount)
    crowded, usual = portions_of(amount, rows * top, limit, slope, True), portions_of(amount, rows * top, limit, slope, False)
    places = jnp.arange(amount)

    def named(lengths, rotation):
        used = int((lengths > 0).sum())
        fixed = max(1, used // 4)
        shifted = fixed + (places - fixed + rotation * (used - fixed)) % max(1, amount - fixed)
        return jnp.zeros((amount,), jnp.int32).at[ranking[jnp.where(places < fixed, places, shifted)]].set(jnp.asarray(lengths, jnp.int32))

    lengths = jnp.where(number % 4 == 0, named(crowded, number // 4), named(usual, number - number // 4 - 1))
    mixed = jax.random.permutation(jax.random.fold_in(own, 3), amount)
    donor, receiver = mixed[0:amount // 2 * 2:2], mixed[1:amount // 2 * 2:2]
    room = jnp.minimum(lengths[donor] - 1, limit - lengths[receiver]) // 2
    room = jnp.where((donor == ranking[0]) | (receiver == ranking[0]) | (lengths[receiver] == 0), 0, jnp.maximum(room, 0))
    shifted = jax.random.randint(jax.random.fold_in(own, 4), (amount // 2,), 0, 1 << 20) % (room + 1)
    lengths = lengths.at[donor].add(-shifted).at[receiver].add(shifted)
    labels = jnp.searchsorted(jnp.cumsum(lengths), jnp.arange(rows * top), side="right").astype(jnp.int32)
    grid = labels.reshape(top, rows).T
    grid = grid[jax.random.permutation(jax.random.fold_in(own, 1), rows)]
    rotation = jax.random.randint(jax.random.fold_in(own, 2), (rows, 1), 0, top)
    return jnp.take_along_axis(grid, (jnp.arange(top)[None, :] + rotation) % top, axis=1)


def portions_of(number_of, total, reach, slope, full):
    loads = [(1 << 20) // math.isqrt(rank ** slope) + 1 for rank in range(1, number_of + 1)]
    largest = reach if full else min(reach, max(-(-total // number_of), total * loads[0] // sum(loads)))
    least = 1 if total - largest >= number_of - 1 else 0
    holding, rest = [largest] + [least] * (number_of - 1), total - largest - least * (number_of - 1)
    while rest > 0:
        free = [i for i in range(1, number_of) if holding[i] < largest] or [i for i in range(1, number_of) if holding[i] < reach]
        pool, left = sum([loads[i] for i in free]), rest
        for i in free:
            more = min(reach - holding[i], max(1, left * loads[i] // pool), rest)
            holding[i] = holding[i] + more
            rest = rest - more
    return np.array(holding)


def setup_inputs(seed: int = 0) -> dict:
    seeds = jax.random.split(jax.random.key(seed), 5)
    particles = draw_particles(jax.random.fold_in(seeds[4], 71), 0)
    templates = draw_templates(jax.random.fold_in(seeds[4], 71), 0)
    classes_keys = jax.random.split(jax.random.fold_in(seeds[2], 1), PARTICLES // PART_DEV)
    classes_turns = jax.random.permutation(jax.random.fold_in(seeds[2], 3), PARTICLES // PART_DEV)
    classes = jax.vmap(lambda own, number: routed_block(jax.random.fold_in(seeds[2], 2), own, number, PART_DEV, CLASSES, 1, CAPACITY, 2))(classes_keys, classes_turns).reshape((PARTICLES, 1))
    rotations = place_ends(jax.random.randint(seeds[3], (PARTICLES,), 0, ROTATIONS), jax.random.fold_in(seeds[3], 1), 0, ROTATIONS - 1).astype(jnp.int32)
    return {"particles": particles, "templates": templates, "classes": classes, "rotations": rotations}


eps = 1e-5


def block_weights(particle_block, class_block, rot_block, flat_templates):
    scores = jnp.dot(particle_block.astype(jnp.float32), flat_templates.T, precision=lax.Precision.HIGHEST)
    target = (class_block * ROTATIONS + rot_block).astype(jnp.int32)
    picked = jnp.take_along_axis(scores, target[:, None], axis=1)[:, 0]
    mean_sq = jnp.mean(scores * scores, axis=1)
    return (picked * picked / (mean_sq + eps)).astype(jnp.bfloat16)


def reference(particles, templates, classes, rotations):
    flat_templates = templates.reshape(CLASSES * ROTATIONS, PIXELS).astype(jnp.float32)
    particle_blocks = particles.reshape(N_TMPL, PART_DEV, PIXELS)
    class_blocks = classes[:, 0].reshape(N_TMPL, PART_DEV)
    rot_blocks = rotations.reshape(N_TMPL, PART_DEV)

    def one_block(running, inputs):
        particle_block, class_block, rot_block = inputs
        block_w = block_weights(particle_block, class_block, rot_block, flat_templates)
        target = (class_block * ROTATIONS + rot_block).astype(jnp.int32)
        weight_f = block_w.astype(jnp.float32)
        contrib = jax.ops.segment_sum(weight_f[:, None] * particle_block.astype(jnp.float32), target, num_segments=CLASSES * ROTATIONS)
        total_part = jax.ops.segment_sum(weight_f, target, num_segments=CLASSES * ROTATIONS)
        return (running[0] + contrib, running[1] + total_part), block_w

    initial = (jnp.zeros((CLASSES * ROTATIONS, PIXELS), jnp.float32), jnp.zeros((CLASSES * ROTATIONS,), jnp.float32))
    (class_sums, totals), weights = lax.scan(one_block, initial, (particle_blocks, class_blocks, rot_blocks))
    class_means = class_sums / jnp.maximum(totals, 1.0)[:, None]
    return class_means.reshape(CLASSES, ROTATIONS, PIXELS), weights.reshape(PARTICLES)
```

```python
import functools

import jax
import jax.numpy as jnp
from jax import lax
from jax.experimental import pallas as pl
from jax.experimental.pallas import tpu as pltpu
from jax.sharding import PartitionSpec as P

CAPACITY = 2
CHUNKS = 4
VIA_SPAN = 1

eps = 1e-05


def place(n):
    me = lax.axis_index("tmpl")
    core = lax.rem(me, 2)
    x = lax.rem(me // 2, 2)
    y = lax.rem(me // 4, 2)
    low = lax.rem(me // 8, 2)
    high = me // 16
    return high, low, y, x, core


def index_of(high, low, y, x, core):
    return (((high * 2 + low) * 2 + y) * 2 + x) * 2 + core


def gather_kernel(n, part_ref, temp_ref, parts_ref, temps_ref, own_sem, ps_sem, pr_sem, ts_sem, tr_sem):
    highs = n // 16
    high, low, y, x, core = place(n)
    pix = part_ref.shape[1]
    width = pix // CHUNKS

    def dev(a, b, c, d, e):
        return {"tmpl": index_of(a, b, c, d, e)}

    to_low = dev(high, 1 - low, y, x, core)
    to_x = dev(high, low, y, 1 - x, core)
    to_y = dev(high, low, 1 - y, x, core)
    to_core = dev(high, low, y, x, 1 - core)
    others = [lax.rem(high + step, highs) for step in range(1, highs)]
    to_high = [dev(o, low, y, x, core) for o in others]
    came_high = [lax.rem(high + highs - step, highs) for step in range(1, highs)]

    barrier = pltpu.get_barrier_semaphore()
    peers = [to_low, to_x, to_y, to_core] + to_high
    for peer in peers:
        pl.semaphore_signal(barrier, inc=1, device_id=peer, device_id_type=pl.DeviceIdType.MESH)
    pl.semaphore_wait(barrier, len(peers))

    def cols(j):
        return pl.ds(j * width, width)

    def send(src, dst, s_sem, r_sem, peer):
        return pltpu.make_async_remote_copy(
            src_ref=src, dst_ref=dst, send_sem=s_sem, recv_sem=r_sem,
            device_id=peer, device_id_type=pl.DeviceIdType.MESH,
        )

    def part(b, d, j):
        return parts_ref.at[b, d, :, cols(j)]

    def temp(a, c, e, j):
        return temps_ref.at[a, c, e, :, cols(j)]

    y0 = highs - 1
    c0 = y0 + highs
    sent = []

    def t_send(kind, src, slot, j, peer):
        cp = send(src, temp(*slot, j), ts_sem.at[kind, j], tr_sem.at[kind, j], peer)
        cp.start()
        sent.append(cp)

    def t_wait(kind, slot, j, peer):
        send(temp(*slot, j), temp(*slot, j), ts_sem.at[kind, j], tr_sem.at[kind, j], peer).wait_recv()

    def p_send(kind, src, slot, j, peer):
        cp = send(src, part(*slot, j), ps_sem.at[kind, j], pr_sem.at[kind, j], peer)
        cp.start()
        sent.append(cp)

    def p_wait(kind, slot, j, peer):
        send(part(*slot, j), part(*slot, j), ps_sem.at[kind, j], pr_sem.at[kind, j], peer).wait_recv()

    for j in range(CHUNKS):
        own_t = temp_ref.at[:, cols(j)]
        own_p = part_ref.at[:, cols(j)]
        for i in range(highs - 1):
            t_send(i, own_t, (high, y, core), j, to_high[i])
        p_send(0, own_p, (low, x), j, to_low)
        p_send(1, own_p, (low, x), j, to_x)
        t_send(y0, own_t, (high, y, core), j, to_y)
        t_send(c0, own_t, (high, y, core), j, to_core)
    own = [
        pltpu.make_async_copy(part_ref, parts_ref.at[low, x], own_sem.at[0]),
        pltpu.make_async_copy(temp_ref, temps_ref.at[high, y, core], own_sem.at[1]),
    ]
    for cp in own:
        cp.start()

    for j in range(CHUNKS):
        for i in range(highs - 1):
            slot = (came_high[i], y, core)
            t_wait(i, slot, j, to_high[i])
            t_send(y0 + 1 + i, temp(*slot, j), slot, j, to_y)
            t_send(c0 + 1 + i, temp(*slot, j), slot, j, to_core)
        p_wait(0, (1 - low, x), j, to_low)
        if j >= VIA_SPAN:
            p_send(2, part(1 - low, x, j), (1 - low, x), j, to_x)
        p_wait(1, (low, 1 - x), j, to_x)
        if j < VIA_SPAN:
            p_send(2, part(low, 1 - x, j), (low, 1 - x), j, to_low)
        slot = (high, 1 - y, core)
        t_wait(y0, slot, j, to_y)
        t_send(c0 + highs, temp(*slot, j), slot, j, to_core)
    for j in range(CHUNKS):
        for i in range(highs - 1):
            slot = (came_high[i], 1 - y, core)
            t_wait(y0 + 1 + i, slot, j, to_y)
            t_send(c0 + highs + 1 + i, temp(*slot, j), slot, j, to_core)
    for j in range(CHUNKS):
        p_wait(2, (1 - low, 1 - x), j, to_low if j < VIA_SPAN else to_x)
        for half in range(2):
            row = y if half == 0 else 1 - y
            t_wait(c0 + half * highs, (high, row, 1 - core), j, to_core)
            for i in range(highs - 1):
                t_wait(c0 + half * highs + 1 + i, (came_high[i], row, 1 - core), j, to_core)
    for cp in own:
        cp.wait()
    for cp in sent:
        cp.wait_send()


def gather_blocks(n, particles, flat_templates):
    highs = n // 16
    rows, pix = particles.shape
    bins = flat_templates.shape[0]
    kinds = 3 * highs - 1 + highs
    total = (rows * 4 + bins * 4 * highs) * pix * 2
    return pl.pallas_call(
        functools.partial(gather_kernel, n),
        out_shape=(
            jax.ShapeDtypeStruct((2, 2, rows, pix), jnp.bfloat16),
            jax.ShapeDtypeStruct((highs, 2, 2, bins, pix), jnp.bfloat16),
        ),
        in_specs=[pl.BlockSpec(memory_space=pl.ANY)] * 2,
        out_specs=[pl.BlockSpec(memory_space=pl.ANY)] * 2,
        scratch_shapes=[
            pltpu.SemaphoreType.DMA((2,)),
            pltpu.SemaphoreType.DMA((3, CHUNKS)),
            pltpu.SemaphoreType.DMA((3, CHUNKS)),
            pltpu.SemaphoreType.DMA((kinds, CHUNKS)),
            pltpu.SemaphoreType.DMA((kinds, CHUNKS)),
        ],
        compiler_params=pltpu.CompilerParams(collective_id=0, has_side_effects=True),
        cost_estimate=pl.CostEstimate(flops=0, bytes_accessed=10 * total, transcendentals=0),
    )(particles, flat_templates)


def body(particles, templates, classes, rotations):
    rows, pix = particles.shape
    local_classes, rot_count, _ = templates.shape
    n = lax.axis_size("tmpl")
    highs = n // 16
    class_count = local_classes * n
    bins = local_classes * rot_count
    high, low, y, x, core = place(n)
    me = lax.axis_index("tmpl")

    class_ids = classes[:, 0]
    row_iota = lax.broadcasted_iota(jnp.int32, (rows, rows), 0)
    col_iota = lax.broadcasted_iota(jnp.int32, (rows, rows), 1)
    same = (class_ids[None, :] == class_ids[:, None]) & (col_iota < row_iota)
    rank = jnp.sum(same.astype(jnp.int32), axis=1)
    slot = class_ids * CAPACITY + rank
    slots = class_count * CAPACITY
    pick = (lax.broadcasted_iota(jnp.int32, (slots, rows), 0) == slot[None, :]).astype(jnp.bfloat16)
    outgoing = jnp.dot(pick, particles, preferred_element_type=jnp.float32).astype(jnp.bfloat16)
    incoming = lax.all_to_all(outgoing, "tmpl", split_axis=0, concat_axis=0, tiled=True)

    label = jnp.stack([slot, rotations], axis=0)
    labels = lax.all_gather(label, "tmpl", axis=0, tiled=False)
    all_slot, all_rot = labels[:, 0], labels[:, 1]
    all_target = (all_slot // CAPACITY) * rot_count + all_rot

    parts, temps = gather_blocks(n, particles, templates.reshape(bins, pix))
    parts = parts.reshape(4 * rows, pix)
    temps = temps.reshape(4 * highs * bins, pix)
    scores = lax.dot_general(parts, temps, (((1,), (1,)), ((), ())), preferred_element_type=jnp.float32)
    if lax.axis_size("dom") > 1:
        scores = lax.psum(scores, "dom")

    grid = all_target.reshape(highs, 2, 2, 2, 2, rows)
    grid = lax.dynamic_index_in_dim(grid, high, 0, keepdims=False)
    grid = lax.dynamic_index_in_dim(grid, y, 1, keepdims=False)
    target = lax.dynamic_index_in_dim(grid, core, 2, keepdims=False).reshape(4 * rows)
    owner = lax.broadcasted_iota(jnp.int32, (highs, 2, 2, bins), 0)
    o_y = lax.broadcasted_iota(jnp.int32, (highs, 2, 2, bins), 1)
    o_c = lax.broadcasted_iota(jnp.int32, (highs, 2, 2, bins), 2)
    o_b = lax.broadcasted_iota(jnp.int32, (highs, 2, 2, bins), 3)
    column = (index_of(owner, low, o_y, x, o_c) * bins + o_b).reshape(1, 4 * highs * bins)
    picked = jnp.sum(jnp.where(column == target[:, None], scores, 0.0), axis=1)
    square = jnp.sum(scores * scores, axis=1)
    both = jnp.stack([picked, square], axis=0)
    groups = [
        [index_of(a, b, c, d, e) for b in range(2) for d in range(2)]
        for a in range(highs) for c in range(2) for e in range(2)
    ]
    both = lax.psum(both, "tmpl", axis_index_groups=groups)
    both = lax.dynamic_index_in_dim(both.reshape(2, 4, rows), low * 2 + x, 1, keepdims=False)
    weights = (both[0] * both[0] / (both[1] / (class_count * rot_count) + eps)).astype(jnp.bfloat16)

    all_w = lax.all_gather(weights, "tmpl", axis=0, tiled=False)
    mine = local_classes * CAPACITY
    here = all_slot - me * mine
    spot = lax.broadcasted_iota(jnp.int32, (n, rows, mine), 2) == here[:, :, None]
    slot_w = jnp.sum(jnp.where(spot, all_w.astype(jnp.float32)[:, :, None], 0.0), axis=1)
    slot_r = jnp.sum(jnp.where(spot, all_rot[:, :, None], 0), axis=1)
    slot_c = lax.broadcasted_iota(jnp.int32, (n, mine), 1) // CAPACITY
    slot_bin = (slot_c * rot_count + slot_r).reshape(1, n * mine)
    bin_iota = lax.broadcasted_iota(jnp.int32, (bins, n * mine), 0)
    mix = jnp.where(bin_iota == slot_bin, slot_w.reshape(1, n * mine), 0.0)
    totals = jnp.sum(mix, axis=1)
    sums = jnp.dot(mix.astype(jnp.bfloat16), incoming, preferred_element_type=jnp.float32)
    means = sums / jnp.maximum(totals, 1.0)[:, None]
    return means.reshape(local_classes, rot_count, pix), weights


def solution(mesh):
    return jax.shard_map(
        body,
        mesh=mesh,
        in_specs=(P("tmpl", "dom"), P("tmpl", None, "dom"), P("tmpl", None), P("tmpl")),
        out_specs=(P("tmpl", None, "dom"), P("tmpl")),
        check_vma=False,
    )
```

```python
import functools

import jax
import jax.numpy as jnp
from jax import lax
from jax.experimental import pallas as pl
from jax.experimental.pallas import tpu as pltpu
from jax.sharding import PartitionSpec as P

CAPACITY = 2
CHUNKS = 4
VIA_SPAN = 0

eps = 1e-05


def place(n):
    me = lax.axis_index("tmpl")
    core = lax.rem(me, 2)
    x = lax.rem(me // 2, 2)
    y = lax.rem(me // 4, 2)
    low = lax.rem(me // 8, 2)
    high = me // 16
    return high, low, y, x, core


def index_of(high, low, y, x, core):
    return (((high * 2 + low) * 2 + y) * 2 + x) * 2 + core


def gather_kernel(n, part_ref, temp_ref, label_ref, parts_ref, temps_ref, labels_ref, own_sem, ps_sem, pr_sem, ts_sem, tr_sem, ls_sem, lr_sem):
    highs = n // 16
    high, low, y, x, core = place(n)
    pix = part_ref.shape[1]
    width = pix // CHUNKS

    def dev(a, b, c, d, e):
        return {"tmpl": index_of(a, b, c, d, e)}

    to_low = dev(high, 1 - low, y, x, core)
    to_x = dev(high, low, y, 1 - x, core)
    to_diag = dev(high, 1 - low, y, 1 - x, core)
    to_y = dev(high, low, 1 - y, x, core)
    to_core = dev(high, low, y, x, 1 - core)
    others = [lax.rem(high + step, highs) for step in range(1, highs)]
    to_high = [dev(o, low, y, x, core) for o in others]
    came_high = [lax.rem(high + highs - step, highs) for step in range(1, highs)]

    barrier = pltpu.get_barrier_semaphore()
    peers = [to_low, to_x, to_diag, to_y, to_core] + to_high
    for peer in peers:
        pl.semaphore_signal(barrier, inc=1, device_id=peer, device_id_type=pl.DeviceIdType.MESH)
    pl.semaphore_wait(barrier, len(peers))

    def cols(j):
        return pl.ds(j * width, width)

    def send(src, dst, s_sem, r_sem, peer):
        return pltpu.make_async_remote_copy(
            src_ref=src, dst_ref=dst, send_sem=s_sem, recv_sem=r_sem,
            device_id=peer, device_id_type=pl.DeviceIdType.MESH,
        )

    def part(b, d, j):
        return parts_ref.at[b, d, :, cols(j)]

    def temp(a, c, e, j):
        return temps_ref.at[a, c, e, :, cols(j)]

    y0 = highs - 1
    c0 = y0 + highs
    sent = []

    def t_send(kind, src, slot, j, peer):
        cp = send(src, temp(*slot, j), ts_sem.at[kind, j], tr_sem.at[kind, j], peer)
        cp.start()
        sent.append(cp)

    def t_wait(kind, slot, j, peer):
        send(temp(*slot, j), temp(*slot, j), ts_sem.at[kind, j], tr_sem.at[kind, j], peer).wait_recv()

    def p_send(kind, src, slot, j, peer):
        cp = send(src, part(*slot, j), ps_sem.at[kind, j], pr_sem.at[kind, j], peer)
        cp.start()
        sent.append(cp)

    def p_wait(kind, slot, j, peer):
        send(part(*slot, j), part(*slot, j), ps_sem.at[kind, j], pr_sem.at[kind, j], peer).wait_recv()

    spot = labels_ref.at[low * 2 + x]
    for i, peer in enumerate((to_low, to_x, to_diag)):
        cp = send(label_ref, spot, ls_sem.at[i], lr_sem.at[i], peer)
        cp.start()
        sent.append(cp)
    for j in range(CHUNKS):
        own_t = temp_ref.at[:, cols(j)]
        own_p = part_ref.at[:, cols(j)]
        for i in range(highs - 1):
            t_send(i, own_t, (high, y, core), j, to_high[i])
        p_send(0, own_p, (low, x), j, to_low)
        p_send(1, own_p, (low, x), j, to_x)
        t_send(y0, own_t, (high, y, core), j, to_y)
        t_send(c0, own_t, (high, y, core), j, to_core)
    own = [
        pltpu.make_async_copy(part_ref, parts_ref.at[low, x], own_sem.at[0]),
        pltpu.make_async_copy(temp_ref, temps_ref.at[high, y, core], own_sem.at[1]),
        pltpu.make_async_copy(label_ref, spot, own_sem.at[2]),
    ]
    for cp in own:
        cp.start()

    for j in range(CHUNKS):
        for i in range(highs - 1):
            slot = (came_high[i], y, core)
            t_wait(i, slot, j, to_high[i])
            t_send(y0 + 1 + i, temp(*slot, j), slot, j, to_y)
            t_send(c0 + 1 + i, temp(*slot, j), slot, j, to_core)
        p_wait(0, (1 - low, x), j, to_low)
        if j >= VIA_SPAN:
            p_send(2, part(1 - low, x, j), (1 - low, x), j, to_x)
        p_wait(1, (low, 1 - x), j, to_x)
        if j < VIA_SPAN:
            p_send(2, part(low, 1 - x, j), (low, 1 - x), j, to_low)
        slot = (high, 1 - y, core)
        t_wait(y0, slot, j, to_y)
        t_send(c0 + highs, temp(*slot, j), slot, j, to_core)
    for j in range(CHUNKS):
        for i in range(highs - 1):
            slot = (came_high[i], 1 - y, core)
            t_wait(y0 + 1 + i, slot, j, to_y)
            t_send(c0 + highs + 1 + i, temp(*slot, j), slot, j, to_core)
    for j in range(CHUNKS):
        p_wait(2, (1 - low, 1 - x), j, to_low if j < VIA_SPAN else to_x)
        for half in range(2):
            row = y if half == 0 else 1 - y
            t_wait(c0 + half * highs, (high, row, 1 - core), j, to_core)
            for i in range(highs - 1):
                t_wait(c0 + half * highs + 1 + i, (came_high[i], row, 1 - core), j, to_core)
    for i, (b, d) in enumerate(((1 - low, x), (low, 1 - x), (1 - low, 1 - x))):
        there = labels_ref.at[b * 2 + d]
        send(there, there, ls_sem.at[i], lr_sem.at[i], to_low).wait_recv()
    for cp in own:
        cp.wait()
    for cp in sent:
        cp.wait_send()


def gather_blocks(n, particles, flat_templates, label):
    highs = n // 16
    rows, pix = particles.shape
    bins = flat_templates.shape[0]
    kinds = 3 * highs - 1 + highs
    total = (rows * 4 + bins * 4 * highs) * pix * 2
    return pl.pallas_call(
        functools.partial(gather_kernel, n),
        out_shape=(
            jax.ShapeDtypeStruct((2, 2, rows, pix), jnp.bfloat16),
            jax.ShapeDtypeStruct((highs, 2, 2, bins, pix), jnp.bfloat16),
            jax.ShapeDtypeStruct((4,) + label.shape, label.dtype),
        ),
        in_specs=[pl.BlockSpec(memory_space=pl.ANY)] * 3,
        out_specs=[pl.BlockSpec(memory_space=pl.ANY)] * 3,
        scratch_shapes=[
            pltpu.SemaphoreType.DMA((3,)),
            pltpu.SemaphoreType.DMA((3, CHUNKS)),
            pltpu.SemaphoreType.DMA((3, CHUNKS)),
            pltpu.SemaphoreType.DMA((kinds, CHUNKS)),
            pltpu.SemaphoreType.DMA((kinds, CHUNKS)),
            pltpu.SemaphoreType.DMA((3,)),
            pltpu.SemaphoreType.DMA((3,)),
        ],
        compiler_params=pltpu.CompilerParams(collective_id=0, has_side_effects=True),
        cost_estimate=pl.CostEstimate(flops=0, bytes_accessed=10 * total, transcendentals=0),
    )(particles, flat_templates, label)


def weigh_kernel(n, columns, both_ref, info_ref, held, as_sem, ar_sem, bs_sem, br_sem):
    highs = n // 16
    high, low, y, x, core = place(n)

    def dev(a, b, c, d, e):
        return {"tmpl": index_of(a, b, c, d, e)}

    near = [(b, d) for b in range(2) for d in range(2) if b or d]
    far = [(a, c, e) for a in range(highs) for c in range(2) for e in range(2) if a or c or e]

    def flip(bit, by):
        return 1 - bit if by else bit

    near_at = [(flip(low, b), flip(x, d)) for b, d in near]
    near_to = [dev(high, b, y, d, core) for b, d in near_at]
    far_to = [dev(lax.rem(high + a, highs), low, flip(y, c), x, flip(core, e)) for a, c, e in far]
    far_at = [(lax.rem(high + highs - a, highs), flip(y, c), flip(core, e)) for a, c, e in far]

    barrier = pltpu.get_barrier_semaphore()
    for peer in near_to + far_to:
        pl.semaphore_signal(barrier, inc=1, device_id=peer, device_id_type=pl.DeviceIdType.MESH)
    pl.semaphore_wait(barrier, len(near_to + far_to))

    def send(src, dst, s_sem, r_sem, peer):
        return pltpu.make_async_remote_copy(
            src_ref=src, dst_ref=dst, send_sem=s_sem, recv_sem=r_sem,
            device_id=peer, device_id_type=pl.DeviceIdType.MESH,
        )

    mine = low * 2 + x
    sent = []
    for i, peer in enumerate(near_to):
        cp = send(both_ref, held.at[mine], as_sem.at[i], ar_sem.at[i], peer)
        cp.start()
        sent.append(cp)
    held[mine] = both_ref[...]
    for i, (b, d) in enumerate(near_at):
        spot = held.at[b * 2 + d]
        send(spot, spot, as_sem.at[i], ar_sem.at[i], near_to[i]).wait_recv()
    total = (held[0] + held[1]) + (held[2] + held[3])
    picked, square = total[:, 0:1], total[:, 1:2]
    weight = (picked * picked / (square / columns + eps)).astype(jnp.bfloat16).astype(jnp.float32)
    row = lax.broadcasted_iota(jnp.int32, total.shape, 1)
    info_ref[high, y, core] = jnp.where(row == 0, weight, both_ref[...])
    own = info_ref.at[high, y, core]
    for i, peer in enumerate(far_to):
        cp = send(own, own, bs_sem.at[i], br_sem.at[i], peer)
        cp.start()
        sent.append(cp)
    for i, at in enumerate(far_at):
        spot = info_ref.at[at[0], at[1], at[2]]
        send(spot, spot, bs_sem.at[i], br_sem.at[i], far_to[i]).wait_recv()
    for cp in sent:
        cp.wait_send()


def weigh_blocks(n, columns, both):
    highs = n // 16
    return pl.pallas_call(
        functools.partial(weigh_kernel, n, columns),
        out_shape=jax.ShapeDtypeStruct((highs, 2, 2) + both.shape, jnp.float32),
        in_specs=[pl.BlockSpec(memory_space=pltpu.VMEM)],
        out_specs=pl.BlockSpec(memory_space=pltpu.VMEM),
        scratch_shapes=[
            pltpu.VMEM((4,) + both.shape, jnp.float32),
            pltpu.SemaphoreType.DMA((3,)),
            pltpu.SemaphoreType.DMA((3,)),
            pltpu.SemaphoreType.DMA((4 * highs - 1,)),
            pltpu.SemaphoreType.DMA((4 * highs - 1,)),
        ],
        compiler_params=pltpu.CompilerParams(collective_id=1, has_side_effects=True),
        cost_estimate=pl.CostEstimate(flops=0, bytes_accessed=20000000, transcendentals=0),
    )(both)


def body(particles, templates, classes, rotations):
    rows, pix = particles.shape
    local_classes, rot_count, _ = templates.shape
    n = lax.axis_size("tmpl")
    highs = n // 16
    class_count = local_classes * n
    bins = local_classes * rot_count
    high, low, y, x, core = place(n)
    me = lax.axis_index("tmpl")

    class_ids = classes[:, 0]
    row_iota = lax.broadcasted_iota(jnp.int32, (rows, rows), 0)
    col_iota = lax.broadcasted_iota(jnp.int32, (rows, rows), 1)
    same = (class_ids[None, :] == class_ids[:, None]) & (col_iota < row_iota)
    rank = jnp.sum(same.astype(jnp.int32), axis=1)
    slot = class_ids * CAPACITY + rank
    slots = class_count * CAPACITY
    pick = (lax.broadcasted_iota(jnp.int32, (slots, rows), 0) == slot[None, :]).astype(jnp.bfloat16)
    early = pix // 4 * 3
    first, second = [
        jnp.dot(pick, part, preferred_element_type=jnp.float32).astype(jnp.bfloat16)
        for part in (particles[:, :early], particles[:, early:])
    ]

    label = jnp.pad(jnp.stack([slot, rotations], axis=0), ((2, 4), (0, 0)))
    first, second, label = lax.optimization_barrier((first, second, label))
    arrived = lax.all_to_all(first, "tmpl", split_axis=0, concat_axis=0, tiled=True)
    flat = templates.transpose(1, 0, 2).reshape(bins, pix)
    parts, temps, labels = gather_blocks(n, particles, flat, label)
    late, labels = lax.optimization_barrier((second, labels))
    late = lax.all_to_all(late, "tmpl", split_axis=0, concat_axis=0, tiled=True)
    parts = parts.reshape(4 * rows, pix)
    temps = temps.reshape(4 * highs * bins, pix)
    scores = lax.dot_general(parts, temps, (((1,), (1,)), ((), ())), preferred_element_type=jnp.float32)
    if lax.axis_size("dom") > 1:
        scores = lax.psum(scores, "dom")

    ids = labels[:, 2] // CAPACITY
    target = ids // local_classes * bins + labels[:, 3] * local_classes + ids % local_classes
    target = target.reshape(4 * rows)
    owner = lax.broadcasted_iota(jnp.int32, (highs, 2, 2, bins), 0)
    o_y = lax.broadcasted_iota(jnp.int32, (highs, 2, 2, bins), 1)
    o_c = lax.broadcasted_iota(jnp.int32, (highs, 2, 2, bins), 2)
    o_b = lax.broadcasted_iota(jnp.int32, (highs, 2, 2, bins), 3)
    column = (index_of(owner, low, o_y, x, o_c) * bins + o_b).reshape(1, 4 * highs * bins)
    picked = jnp.sum(jnp.where(column == target[:, None], scores, 0.0), axis=1)
    square = jnp.sum(scores * scores, axis=1)
    both = jnp.stack([picked.reshape(4, rows), square.reshape(4, rows)], axis=1)
    both = jnp.pad(both, ((0, 0), (0, 6), (0, 0))) + labels.astype(jnp.float32)
    info = weigh_blocks(n, float(class_count * rot_count), both)
    own = lax.dynamic_slice(info, (high, y, core, low * 2 + x, 0, 0), (1, 1, 1, 1, 1, rows))
    weights = own.reshape(rows).astype(jnp.bfloat16)

    info = info.reshape(highs, 2, 2, 2, 2, 8, rows).transpose(0, 3, 1, 4, 2, 5, 6).reshape(n, 8, rows)
    all_w, all_slot, all_rot = info[:, 0], info[:, 2].astype(jnp.int32), info[:, 3].astype(jnp.int32)
    mine = local_classes * CAPACITY
    here = all_slot - me * mine
    spot = lax.broadcasted_iota(jnp.int32, (n, rows, mine), 2) == here[:, :, None]
    slot_w = jnp.sum(jnp.where(spot, all_w[:, :, None], 0.0), axis=1)
    slot_r = jnp.sum(jnp.where(spot, all_rot[:, :, None], 0), axis=1)
    slot_c = lax.broadcasted_iota(jnp.int32, (n, mine), 1) // CAPACITY
    slot_bin = (slot_r * local_classes + slot_c).reshape(1, n * mine)
    bin_iota = lax.broadcasted_iota(jnp.int32, (bins, n * mine), 0)
    mix = jnp.where(bin_iota == slot_bin, slot_w.reshape(1, n * mine), 0.0)
    totals = jnp.sum(mix, axis=1)
    mix = mix.astype(jnp.bfloat16)
    least = jnp.maximum(totals, 1.0)[:, None]
    means = [jnp.dot(mix, part, preferred_element_type=jnp.float32) / least for part in (arrived, late)]
    means = [part.reshape(rot_count, local_classes, part.shape[1]) for part in means]
    return jnp.concatenate(means, axis=2).transpose(1, 0, 2), weights


def solution(mesh):
    return jax.shard_map(
        body,
        mesh=mesh,
        in_specs=(P("tmpl", "dom"), P("tmpl", None, "dom"), P("tmpl", None), P("tmpl")),
        out_specs=(P("tmpl", None, "dom"), P("tmpl")),
        check_vma=False,
    )
```

```python
import functools

import jax
import jax.numpy as jnp
from jax import lax
from jax.experimental import pallas as pl
from jax.experimental.pallas import tpu as pltpu
from jax.sharding import PartitionSpec as P

CHUNKS = 4
VIA_SPAN = 1
WIDTH = 1024

eps = 1e-05


def place(n):
    me = lax.axis_index("tmpl")
    core = lax.rem(me, 2)
    x = lax.rem(me // 2, 2)
    y = lax.rem(me // 4, 2)
    low = lax.rem(me // 8, 2)
    high = me // 16
    return high, low, y, x, core


def index_of(high, low, y, x, core):
    return (((high * 2 + low) * 2 + y) * 2 + x) * 2 + core


def gather_kernel(n, part_ref, temp_ref, label_ref, parts_ref, sibs_ref, temps_ref, labels_ref, own_sem, ps_sem, pr_sem, ts_sem, tr_sem, ls_sem, lr_sem):
    highs = n // 16
    high, low, y, x, core = place(n)
    pix = part_ref.shape[1]
    width = pix // CHUNKS

    def dev(a, b, c, d, e):
        return {"tmpl": index_of(a, b, c, d, e)}

    to_low = dev(high, 1 - low, y, x, core)
    to_x = dev(high, low, y, 1 - x, core)
    to_diag = dev(high, 1 - low, y, 1 - x, core)
    to_y = dev(high, low, 1 - y, x, core)
    to_core = dev(high, low, y, x, 1 - core)
    others = [lax.rem(high + step, highs) for step in range(1, highs)]
    to_high = [dev(o, low, y, x, core) for o in others]
    came_high = [lax.rem(high + highs - step, highs) for step in range(1, highs)]

    barrier = pltpu.get_barrier_semaphore()
    peers = [to_low, to_x, to_diag, to_y, to_core] + to_high
    for peer in peers:
        pl.semaphore_signal(barrier, inc=1, device_id=peer, device_id_type=pl.DeviceIdType.MESH)
    pl.semaphore_wait(barrier, len(peers))

    def cols(j):
        return pl.ds(j * width, width)

    def send(src, dst, s_sem, r_sem, peer):
        return pltpu.make_async_remote_copy(
            src_ref=src, dst_ref=dst, send_sem=s_sem, recv_sem=r_sem,
            device_id=peer, device_id_type=pl.DeviceIdType.MESH,
        )

    def part(b, d, j):
        return parts_ref.at[b, d, :, cols(j)]

    def temp(a, c, e, j):
        return temps_ref.at[a, c, e, :, cols(j)]

    y0 = highs - 1
    c0 = y0 + highs
    sent = []

    def t_send(kind, src, slot, j, peer):
        cp = send(src, temp(*slot, j), ts_sem.at[kind, j], tr_sem.at[kind, j], peer)
        cp.start()
        sent.append(cp)

    def t_wait(kind, slot, j, peer):
        send(temp(*slot, j), temp(*slot, j), ts_sem.at[kind, j], tr_sem.at[kind, j], peer).wait_recv()

    def p_send(kind, src, slot, j, peer):
        cp = send(src, part(*slot, j), ps_sem.at[kind, j], pr_sem.at[kind, j], peer)
        cp.start()
        sent.append(cp)

    def p_share(i, src, slot, j):
        there = sibs_ref.at[slot[0], slot[1], :, cols(j)]
        cp = send(src, there, ps_sem.at[3 + i, j], pr_sem.at[3 + i, j], to_core)
        cp.start()
        sent.append(cp)

    def p_wait(kind, slot, j, peer):
        send(part(*slot, j), part(*slot, j), ps_sem.at[kind, j], pr_sem.at[kind, j], peer).wait_recv()

    spot = labels_ref.at[low * 2 + x]
    for i, peer in enumerate((to_low, to_x, to_diag)):
        cp = send(label_ref, spot, ls_sem.at[i], lr_sem.at[i], peer)
        cp.start()
        sent.append(cp)
    for j in range(CHUNKS):
        own_t = temp_ref.at[:, cols(j)]
        own_p = part_ref.at[:, cols(j)]
        for i in range(highs - 1):
            t_send(i, own_t, (high, y, core), j, to_high[i])
        p_send(0, own_p, (low, x), j, to_low)
        p_send(1, own_p, (low, x), j, to_x)
        p_share(0, own_p, (low, x), j)
        t_send(y0, own_t, (high, y, core), j, to_y)
        t_send(c0, own_t, (high, y, core), j, to_core)
    own = [
        pltpu.make_async_copy(part_ref, parts_ref.at[low, x], own_sem.at[0]),
        pltpu.make_async_copy(temp_ref, temps_ref.at[high, y, core], own_sem.at[1]),
        pltpu.make_async_copy(label_ref, spot, own_sem.at[2]),
    ]
    for cp in own:
        cp.start()

    for j in range(CHUNKS):
        for i in range(highs - 1):
            slot = (came_high[i], y, core)
            t_wait(i, slot, j, to_high[i])
            t_send(y0 + 1 + i, temp(*slot, j), slot, j, to_y)
            t_send(c0 + 1 + i, temp(*slot, j), slot, j, to_core)
        p_wait(0, (1 - low, x), j, to_low)
        p_share(1, part(1 - low, x, j), (1 - low, x), j)
        if j >= VIA_SPAN:
            p_send(2, part(1 - low, x, j), (1 - low, x), j, to_x)
        p_wait(1, (low, 1 - x), j, to_x)
        p_share(2, part(low, 1 - x, j), (low, 1 - x), j)
        if j < VIA_SPAN:
            p_send(2, part(low, 1 - x, j), (low, 1 - x), j, to_low)
        slot = (high, 1 - y, core)
        t_wait(y0, slot, j, to_y)
        t_send(c0 + highs, temp(*slot, j), slot, j, to_core)
    for j in range(CHUNKS):
        for i in range(highs - 1):
            slot = (came_high[i], 1 - y, core)
            t_wait(y0 + 1 + i, slot, j, to_y)
            t_send(c0 + highs + 1 + i, temp(*slot, j), slot, j, to_core)
    for j in range(CHUNKS):
        p_wait(2, (1 - low, 1 - x), j, to_low if j < VIA_SPAN else to_x)
        p_share(3, part(1 - low, 1 - x, j), (1 - low, 1 - x), j)
        for half in range(2):
            row = y if half == 0 else 1 - y
            t_wait(c0 + half * highs, (high, row, 1 - core), j, to_core)
            for i in range(highs - 1):
                t_wait(c0 + half * highs + 1 + i, (came_high[i], row, 1 - core), j, to_core)
    for i, at in enumerate(((low, x), (1 - low, x), (low, 1 - x), (1 - low, 1 - x))):
        for j in range(CHUNKS):
            there = sibs_ref.at[at[0], at[1], :, cols(j)]
            send(there, there, ps_sem.at[3 + i, j], pr_sem.at[3 + i, j], to_core).wait_recv()
    for i, (b, d) in enumerate(((1 - low, x), (low, 1 - x), (1 - low, 1 - x))):
        there = labels_ref.at[b * 2 + d]
        send(there, there, ls_sem.at[i], lr_sem.at[i], to_low).wait_recv()
    for cp in own:
        cp.wait()
    for cp in sent:
        cp.wait_send()


def gather_blocks(n, particles, flat_templates, label):
    highs = n // 16
    rows, pix = particles.shape
    bins = flat_templates.shape[0]
    kinds = 3 * highs - 1 + highs
    total = (rows * 4 + bins * 4 * highs) * pix * 2
    return pl.pallas_call(
        functools.partial(gather_kernel, n),
        out_shape=(
            jax.ShapeDtypeStruct((2, 2, rows, pix), jnp.bfloat16),
            jax.ShapeDtypeStruct((2, 2, rows, pix), jnp.bfloat16),
            jax.ShapeDtypeStruct((highs, 2, 2, bins, pix), jnp.bfloat16),
            jax.ShapeDtypeStruct((4,) + label.shape, label.dtype),
        ),
        in_specs=[pl.BlockSpec(memory_space=pl.ANY)] * 3,
        out_specs=[pl.BlockSpec(memory_space=pl.ANY)] * 4,
        scratch_shapes=[
            pltpu.SemaphoreType.DMA((3,)),
            pltpu.SemaphoreType.DMA((7, CHUNKS)),
            pltpu.SemaphoreType.DMA((7, CHUNKS)),
            pltpu.SemaphoreType.DMA((kinds, CHUNKS)),
            pltpu.SemaphoreType.DMA((kinds, CHUNKS)),
            pltpu.SemaphoreType.DMA((3,)),
            pltpu.SemaphoreType.DMA((3,)),
        ],
        compiler_params=pltpu.CompilerParams(collective_id=0, has_side_effects=True),
        cost_estimate=pl.CostEstimate(flops=0, bytes_accessed=10 * total, transcendentals=0),
    )(particles, flat_templates, label)


def weigh_kernel(n, columns, both_ref, info_ref, held, as_sem, ar_sem, bs_sem, br_sem):
    highs = n // 16
    high, low, y, x, core = place(n)

    def dev(a, b, c, d, e):
        return {"tmpl": index_of(a, b, c, d, e)}

    near = [(b, d) for b in range(2) for d in range(2) if b or d]
    far = [(a, c, e) for a in range(highs) for c in range(2) for e in range(2) if a or c or e]

    def flip(bit, by):
        return 1 - bit if by else bit

    near_at = [(flip(low, b), flip(x, d)) for b, d in near]
    near_to = [dev(high, b, y, d, core) for b, d in near_at]
    far_to = [dev(lax.rem(high + a, highs), low, flip(y, c), x, flip(core, e)) for a, c, e in far]
    far_at = [(lax.rem(high + highs - a, highs), flip(y, c), flip(core, e)) for a, c, e in far]

    barrier = pltpu.get_barrier_semaphore()
    for peer in near_to + far_to:
        pl.semaphore_signal(barrier, inc=1, device_id=peer, device_id_type=pl.DeviceIdType.MESH)
    pl.semaphore_wait(barrier, len(near_to + far_to))

    def send(src, dst, s_sem, r_sem, peer):
        return pltpu.make_async_remote_copy(
            src_ref=src, dst_ref=dst, send_sem=s_sem, recv_sem=r_sem,
            device_id=peer, device_id_type=pl.DeviceIdType.MESH,
        )

    mine = low * 2 + x
    sent = []
    for i, peer in enumerate(near_to):
        cp = send(both_ref, held.at[mine], as_sem.at[i], ar_sem.at[i], peer)
        cp.start()
        sent.append(cp)
    held[mine] = both_ref[...]
    for i, (b, d) in enumerate(near_at):
        spot = held.at[b * 2 + d]
        send(spot, spot, as_sem.at[i], ar_sem.at[i], near_to[i]).wait_recv()
    total = (held[0] + held[1]) + (held[2] + held[3])
    picked, square = total[:, 0:1], total[:, 1:2]
    weight = (picked * picked / (square / columns + eps)).astype(jnp.bfloat16).astype(jnp.float32)
    row = lax.broadcasted_iota(jnp.int32, total.shape, 1)
    info_ref[high, y, core] = jnp.where(row == 0, weight, both_ref[...])
    own = info_ref.at[high, y, core]
    for i, peer in enumerate(far_to):
        cp = send(own, own, bs_sem.at[i], br_sem.at[i], peer)
        cp.start()
        sent.append(cp)
    for i, at in enumerate(far_at):
        spot = info_ref.at[at[0], at[1], at[2]]
        send(spot, spot, bs_sem.at[i], br_sem.at[i], far_to[i]).wait_recv()
    for cp in sent:
        cp.wait_send()


def weigh_blocks(n, columns, both):
    highs = n // 16
    return pl.pallas_call(
        functools.partial(weigh_kernel, n, columns),
        out_shape=jax.ShapeDtypeStruct((highs, 2, 2) + both.shape, jnp.float32),
        in_specs=[pl.BlockSpec(memory_space=pltpu.VMEM)],
        out_specs=pl.BlockSpec(memory_space=pltpu.VMEM),
        scratch_shapes=[
            pltpu.VMEM((4,) + both.shape, jnp.float32),
            pltpu.SemaphoreType.DMA((3,)),
            pltpu.SemaphoreType.DMA((3,)),
            pltpu.SemaphoreType.DMA((4 * highs - 1,)),
            pltpu.SemaphoreType.DMA((4 * highs - 1,)),
        ],
        compiler_params=pltpu.CompilerParams(collective_id=1, has_side_effects=True),
        cost_estimate=pl.CostEstimate(flops=0, bytes_accessed=20000000, transcendentals=0),
    )(both)


def sum_kernel(n, mix_ref, least_ref, parts_ref, sibs_ref, out_ref, buf, y_out, y_in, kept, h_out, h_in,
               buf_sem, ys_sem, yr_sem, hs_sem, hr_sem):
    highs = n // 16
    high, low, y, x, core = place(n)
    bins = out_ref.shape[0]
    span = highs * bins
    rows = parts_ref.shape[0]
    steps = out_ref.shape[1] // WIDTH

    def dev(a, c):
        return {"tmpl": index_of(a, low, c, x, core)}

    to_y = dev(high, 1 - y)
    to_high = [dev(lax.rem(high + k, highs), y) for k in range(1, highs)]

    barrier = pltpu.get_barrier_semaphore()
    for peer in [to_y] + to_high:
        pl.semaphore_signal(barrier, inc=1, device_id=peer, device_id_type=pl.DeviceIdType.MESH)
    pl.semaphore_wait(barrier, highs)

    def load(j, slot):
        at = pl.ds(pl.multiple_of(j * WIDTH, WIDTH), WIDTH)
        return (
            pltpu.make_async_copy(parts_ref.at[:, at], buf.at[slot, 0], buf_sem.at[slot, 0]),
            pltpu.make_async_copy(sibs_ref.at[:, at], buf.at[slot, 1], buf_sem.at[slot, 1]),
        )

    def send_y(j):
        return pltpu.make_async_remote_copy(
            src_ref=y_out.at[j], dst_ref=y_in.at[j], send_sem=ys_sem.at[j], recv_sem=yr_sem.at[j],
            device_id=to_y, device_id_type=pl.DeviceIdType.MESH,
        )

    def send_h(j, k):
        return pltpu.make_async_remote_copy(
            src_ref=h_out.at[j, k - 1], dst_ref=h_in.at[j, k - 1],
            send_sem=hs_sem.at[j, k - 1], recv_sem=hr_sem.at[j, k - 1],
            device_id=to_high[k - 1], device_id_type=pl.DeviceIdType.MESH,
        )

    for cp in load(0, 0):
        cp.start()

    def form(j, carry):
        slot = lax.rem(j, 2)

        @pl.when(j + 1 < steps)
        def _():
            for cp in load(j + 1, 1 - slot):
                cp.start()

        for cp in load(j, slot):
            cp.wait()
        mix = mix_ref[...]
        both = jnp.dot(mix[:, :rows], buf[slot, 0], preferred_element_type=jnp.float32)
        both += jnp.dot(mix[:, rows:], buf[slot, 1], preferred_element_type=jnp.float32)
        y_out[j] = both[:span].astype(jnp.bfloat16)
        kept[j] = both[span:]
        send_y(j).start()
        return carry

    def merge(j, carry):
        send_y(j).wait_recv()
        total = kept[j] + y_in[j].astype(jnp.float32)
        kept[j] = total
        for k in range(1, highs):
            h_out[j, k - 1] = total[k * bins:(k + 1) * bins].astype(jnp.bfloat16)
            send_h(j, k).start()
        return carry

    def finish(j, carry):
        total = kept[j][:bins]
        for k in range(1, highs):
            send_h(j, k).wait_recv()
            total += h_in[j, k - 1].astype(jnp.float32)
        out_ref[:, pl.ds(pl.multiple_of(j * WIDTH, WIDTH), WIDTH)] = total / least_ref[:, 0:1]
        return carry

    def drain(j, carry):
        send_y(j).wait_send()
        for k in range(1, highs):
            send_h(j, k).wait_send()
        return carry

    for stage in (form, merge, finish, drain):
        lax.fori_loop(0, steps, stage, 0)


def sum_blocks(n, mix, least, parts, sibs):
    highs = n // 16
    rows, pix = parts.shape
    bins = least.shape[0]
    steps = pix // WIDTH
    anywhere = pl.BlockSpec(memory_space=pl.ANY)
    local = pl.BlockSpec(memory_space=pltpu.VMEM)
    return pl.pallas_call(
        functools.partial(sum_kernel, n),
        out_shape=jax.ShapeDtypeStruct((bins, pix), jnp.float32),
        in_specs=[local, local, anywhere, anywhere],
        out_specs=local,
        scratch_shapes=[
            pltpu.VMEM((2, 2, rows, WIDTH), jnp.bfloat16),
            pltpu.VMEM((steps, highs * bins, WIDTH), jnp.bfloat16),
            pltpu.VMEM((steps, highs * bins, WIDTH), jnp.bfloat16),
            pltpu.VMEM((steps, highs * bins, WIDTH), jnp.float32),
            pltpu.VMEM((steps, highs - 1, bins, WIDTH), jnp.bfloat16),
            pltpu.VMEM((steps, highs - 1, bins, WIDTH), jnp.bfloat16),
            pltpu.SemaphoreType.DMA((2, 2)),
            pltpu.SemaphoreType.DMA((steps,)),
            pltpu.SemaphoreType.DMA((steps,)),
            pltpu.SemaphoreType.DMA((steps, highs - 1)),
            pltpu.SemaphoreType.DMA((steps, highs - 1)),
        ],
        compiler_params=pltpu.CompilerParams(
            collective_id=2, has_side_effects=True, vmem_limit_bytes=48 * 1024 * 1024
        ),
        cost_estimate=pl.CostEstimate(
            flops=4 * rows * mix.shape[0] * pix, bytes_accessed=4 * rows * pix, transcendentals=0
        ),
    )(mix, least, parts, sibs)


def body(particles, templates, classes, rotations):
    rows, pix = particles.shape
    local_classes, rot_count, _ = templates.shape
    n = lax.axis_size("tmpl")
    highs = n // 16
    bins = local_classes * rot_count
    total_bins = bins * n
    high, low, y, x, core = place(n)
    me = lax.axis_index("tmpl")

    class_ids = classes[:, 0]
    target = class_ids // local_classes * bins + rotations * local_classes + class_ids % local_classes
    label = jnp.pad(target[None], ((2, 5), (0, 0)))
    flat = templates.transpose(1, 0, 2).reshape(bins, pix)
    parts, sibs, temps, labels = gather_blocks(n, particles, flat, label)
    parts = parts.reshape(4 * rows, pix)
    sibs = sibs.reshape(4 * rows, pix)
    temps = temps.reshape(4 * highs * bins, pix)
    scores = lax.dot_general(parts, temps, (((1,), (1,)), ((), ())), preferred_element_type=jnp.float32)
    if lax.axis_size("dom") > 1:
        scores = lax.psum(scores, "dom")

    shape = (highs, 2, 2, bins)
    owner, o_y, o_c, o_b = [lax.broadcasted_iota(jnp.int32, shape, i) for i in range(4)]
    column = (index_of(owner, low, o_y, x, o_c) * bins + o_b).reshape(1, 4 * highs * bins)
    near = labels[:, 2].reshape(4 * rows)
    picked = jnp.sum(jnp.where(column == near[:, None], scores, 0.0), axis=1)
    square = jnp.sum(scores * scores, axis=1)
    both = jnp.stack([picked.reshape(4, rows), square.reshape(4, rows)], axis=1)
    both = jnp.pad(both, ((0, 0), (0, 6), (0, 0))) + labels.astype(jnp.float32)
    info = weigh_blocks(n, float(total_bins), both)

    def rows_of(e):
        block = lax.dynamic_slice(info, (high, y, e, 0, 0, 0), (1, 1, 1, 4, 8, rows))
        return block.reshape(4, 8, rows)

    here = rows_of(core)
    weights = lax.dynamic_index_in_dim(here, low * 2 + x, 0, keepdims=False)[0].astype(jnp.bfloat16)
    chip = jnp.stack([here, rows_of(1 - core)])
    chip_w = chip[:, :, 0].reshape(1, 8 * rows)
    chip_t = chip[:, :, 2].astype(jnp.int32).reshape(1, 8 * rows)
    shape = (2, highs, bins)
    flip, ahead, o_b = [lax.broadcasted_iota(jnp.int32, shape, i) for i in range(3)]
    o_y = jnp.where(flip == 0, 1 - y, y)
    wanted = index_of((high + ahead) % highs, low, o_y, x, core) * bins + o_b
    mix = jnp.where(wanted.reshape(2 * highs * bins, 1) == chip_t, chip_w, 0.0).astype(jnp.bfloat16)

    all_w = info[..., 0, :].reshape(1, n * rows)
    all_t = info[..., 2, :].astype(jnp.int32).reshape(1, n * rows)
    own = me * bins + lax.broadcasted_iota(jnp.int32, (bins, 1), 0)
    totals = jnp.sum(jnp.where(own == all_t, all_w, 0.0), axis=1)
    least = jnp.broadcast_to(jnp.maximum(totals, 1.0)[:, None], (bins, 128))
    means = sum_blocks(n, mix, least, parts, sibs)
    return means.reshape(rot_count, local_classes, pix).transpose(1, 0, 2), weights


def solution(mesh):
    return jax.shard_map(
        body,
        mesh=mesh,
        in_specs=(P("tmpl", "dom"), P("tmpl", None, "dom"), P("tmpl", None), P("tmpl")),
        out_specs=(P("tmpl", None, "dom"), P("tmpl")),
        check_vma=False,
    )
```

```python
import functools

import jax
import jax.numpy as jnp
from jax import lax
from jax.experimental import pallas as pl
from jax.experimental.pallas import tpu as pltpu
from jax.sharding import PartitionSpec as P

CHUNKS = 8
VIA_SPAN = 2
WIDTH = 1024

eps = 1e-05


def place(n):
    me = lax.axis_index("tmpl")
    core = lax.rem(me, 2)
    x = lax.rem(me // 2, 2)
    y = lax.rem(me // 4, 2)
    low = lax.rem(me // 8, 2)
    high = me // 16
    return high, low, y, x, core


def index_of(high, low, y, x, core):
    return (((high * 2 + low) * 2 + y) * 2 + x) * 2 + core


def gather_kernel(n, part_ref, temp_ref, label_ref, parts_ref, sibs_ref, temps_ref, labels_ref, score_ref, p_buf, t_buf, buf_sem, own_sem, ps_sem, pr_sem, ts_sem, tr_sem, ls_sem, lr_sem):
    highs = n // 16
    high, low, y, x, core = place(n)
    pix = part_ref.shape[1]
    width = pix // CHUNKS

    def dev(a, b, c, d, e):
        return {"tmpl": index_of(a, b, c, d, e)}

    to_low = dev(high, 1 - low, y, x, core)
    to_x = dev(high, low, y, 1 - x, core)
    to_diag = dev(high, 1 - low, y, 1 - x, core)
    to_y = dev(high, low, 1 - y, x, core)
    to_core = dev(high, low, y, x, 1 - core)
    others = [lax.rem(high + step, highs) for step in range(1, highs)]
    to_high = [dev(o, low, y, x, core) for o in others]
    came_high = [lax.rem(high + highs - step, highs) for step in range(1, highs)]

    barrier = pltpu.get_barrier_semaphore()
    peers = [to_low, to_x, to_diag, to_y, to_core] + to_high
    for peer in peers:
        pl.semaphore_signal(barrier, inc=1, device_id=peer, device_id_type=pl.DeviceIdType.MESH)
    pl.semaphore_wait(barrier, len(peers))

    def cols(j):
        return pl.ds(j * width, width)

    def send(src, dst, s_sem, r_sem, peer):
        return pltpu.make_async_remote_copy(
            src_ref=src, dst_ref=dst, send_sem=s_sem, recv_sem=r_sem,
            device_id=peer, device_id_type=pl.DeviceIdType.MESH,
        )

    def part(b, d, j):
        return parts_ref.at[b, d, :, cols(j)]

    def temp(a, c, e, j):
        return temps_ref.at[a, c, e, :, cols(j)]

    y0 = highs - 1
    c0 = y0 + highs
    sent = []

    def t_send(kind, src, slot, j, peer):
        cp = send(src, temp(*slot, j), ts_sem.at[kind, j], tr_sem.at[kind, j], peer)
        cp.start()
        sent.append(cp)

    def t_wait(kind, slot, j, peer):
        send(temp(*slot, j), temp(*slot, j), ts_sem.at[kind, j], tr_sem.at[kind, j], peer).wait_recv()

    def p_send(kind, src, slot, j, peer):
        cp = send(src, part(*slot, j), ps_sem.at[kind, j], pr_sem.at[kind, j], peer)
        cp.start()
        sent.append(cp)

    def p_share(i, src, slot, j):
        there = sibs_ref.at[slot[0], slot[1], :, cols(j)]
        cp = send(src, there, ps_sem.at[3 + i, j], pr_sem.at[3 + i, j], to_core)
        cp.start()
        sent.append(cp)

    def p_wait(kind, slot, j, peer):
        send(part(*slot, j), part(*slot, j), ps_sem.at[kind, j], pr_sem.at[kind, j], peer).wait_recv()

    spot = labels_ref.at[low * 2 + x]
    for i, peer in enumerate((to_low, to_x, to_diag)):
        cp = send(label_ref, spot, ls_sem.at[i], lr_sem.at[i], peer)
        cp.start()
        sent.append(cp)
    for j in range(CHUNKS):
        own_t = temp_ref.at[:, cols(j)]
        own_p = part_ref.at[:, cols(j)]
        for i in range(highs - 1):
            t_send(i, own_t, (high, y, core), j, to_high[i])
        p_send(0, own_p, (low, x), j, to_low)
        p_send(1, own_p, (low, x), j, to_x)
        p_share(0, own_p, (low, x), j)
        t_send(y0, own_t, (high, y, core), j, to_y)
        t_send(c0, own_t, (high, y, core), j, to_core)
    own = [
        pltpu.make_async_copy(part_ref, parts_ref.at[low, x], own_sem.at[0]),
        pltpu.make_async_copy(temp_ref, temps_ref.at[high, y, core], own_sem.at[1]),
        pltpu.make_async_copy(label_ref, spot, own_sem.at[2]),
    ]
    for cp in own:
        cp.start()

    def first_hop(j):
        for i in range(highs - 1):
            slot = (came_high[i], y, core)
            t_wait(i, slot, j, to_high[i])
            t_send(y0 + 1 + i, temp(*slot, j), slot, j, to_y)
            t_send(c0 + 1 + i, temp(*slot, j), slot, j, to_core)
        p_wait(0, (1 - low, x), j, to_low)
        if j >= VIA_SPAN:
            p_send(2, part(1 - low, x, j), (1 - low, x), j, to_x)
        p_share(1, part(1 - low, x, j), (1 - low, x), j)
        p_wait(1, (low, 1 - x), j, to_x)
        if j < VIA_SPAN:
            p_send(2, part(low, 1 - x, j), (low, 1 - x), j, to_low)
        p_share(2, part(low, 1 - x, j), (low, 1 - x), j)
        slot = (high, 1 - y, core)
        t_wait(y0, slot, j, to_y)
        t_send(c0 + highs, temp(*slot, j), slot, j, to_core)

    def second_hop(j):
        for i in range(highs - 1):
            slot = (came_high[i], 1 - y, core)
            t_wait(y0 + 1 + i, slot, j, to_y)
            t_send(c0 + highs + 1 + i, temp(*slot, j), slot, j, to_core)
        p_wait(2, (1 - low, 1 - x), j, to_low if j < VIA_SPAN else to_x)
        p_share(3, part(1 - low, 1 - x, j), (1 - low, 1 - x), j)

    def loads(j):
        return (
            pltpu.make_async_copy(parts_ref.at[:, :, :, cols(j)], p_buf.at[j % 2], buf_sem.at[j % 2, 0]),
            pltpu.make_async_copy(temps_ref.at[:, :, :, :, cols(j)], t_buf.at[j % 2], buf_sem.at[j % 2, 1]),
        )

    def third_hop(j):
        for half in range(2):
            row = y if half == 0 else 1 - y
            t_wait(c0 + half * highs, (high, row, 1 - core), j, to_core)
            for i in range(highs - 1):
                t_wait(c0 + half * highs + 1 + i, (came_high[i], row, 1 - core), j, to_core)
        if j == 0:
            own[0].wait()
            own[1].wait()
        for cp in loads(j):
            cp.start()

    def score(j):
        for cp in loads(j):
            cp.wait()
        left = p_buf[j % 2].reshape(4 * part_ref.shape[0], width)
        slots = [(a, c, e) for a in range(highs) for c in range(2) for e in range(2)]
        right = jnp.concatenate([t_buf[(j % 2,) + at] for at in slots], axis=0)
        more = lax.dot_general(left, right, (((1,), (1,)), ((), ())), preferred_element_type=jnp.float32)
        if j == 0:
            score_ref[...] = more
        else:
            score_ref[...] += more

    for j in range(CHUNKS + 3):
        for late, stage in enumerate((first_hop, second_hop, third_hop, score)):
            if 0 <= j - late < CHUNKS:
                stage(j - late)
    for i, at in enumerate(((low, x), (1 - low, x), (low, 1 - x), (1 - low, 1 - x))):
        for j in range(CHUNKS):
            there = sibs_ref.at[at[0], at[1], :, cols(j)]
            send(there, there, ps_sem.at[3 + i, j], pr_sem.at[3 + i, j], to_core).wait_recv()
    for i, (b, d) in enumerate(((1 - low, x), (low, 1 - x), (1 - low, 1 - x))):
        there = labels_ref.at[b * 2 + d]
        send(there, there, ls_sem.at[i], lr_sem.at[i], to_low).wait_recv()
    own[2].wait()
    for cp in sent:
        cp.wait_send()


def gather_blocks(n, particles, flat_templates, label):
    highs = n // 16
    rows, pix = particles.shape
    bins = flat_templates.shape[0]
    kinds = 3 * highs - 1 + highs
    total = (rows * 4 + bins * 4 * highs) * pix * 2
    return pl.pallas_call(
        functools.partial(gather_kernel, n),
        out_shape=(
            jax.ShapeDtypeStruct((2, 2, rows, pix), jnp.bfloat16),
            jax.ShapeDtypeStruct((2, 2, rows, pix), jnp.bfloat16),
            jax.ShapeDtypeStruct((highs, 2, 2, bins, pix), jnp.bfloat16),
            jax.ShapeDtypeStruct((4,) + label.shape, label.dtype),
            jax.ShapeDtypeStruct((4 * rows, 4 * highs * bins), jnp.float32),
        ),
        in_specs=[pl.BlockSpec(memory_space=pl.ANY)] * 3,
        out_specs=[pl.BlockSpec(memory_space=pl.ANY)] * 4 + [pl.BlockSpec(memory_space=pltpu.VMEM)],
        scratch_shapes=[
            pltpu.VMEM((2, 2, 2, rows, pix // CHUNKS), jnp.bfloat16),
            pltpu.VMEM((2, highs, 2, 2, bins, pix // CHUNKS), jnp.bfloat16),
            pltpu.SemaphoreType.DMA((2, 2)),
            pltpu.SemaphoreType.DMA((3,)),
            pltpu.SemaphoreType.DMA((7, CHUNKS)),
            pltpu.SemaphoreType.DMA((7, CHUNKS)),
            pltpu.SemaphoreType.DMA((kinds, CHUNKS)),
            pltpu.SemaphoreType.DMA((kinds, CHUNKS)),
            pltpu.SemaphoreType.DMA((3,)),
            pltpu.SemaphoreType.DMA((3,)),
        ],
        compiler_params=pltpu.CompilerParams(
            collective_id=0, has_side_effects=True, vmem_limit_bytes=40 * 1024 * 1024
        ),
        cost_estimate=pl.CostEstimate(flops=0, bytes_accessed=10 * total, transcendentals=0),
    )(particles, flat_templates, label)


def weigh_kernel(n, columns, both_ref, info_ref, held, as_sem, ar_sem, bs_sem, br_sem):
    highs = n // 16
    high, low, y, x, core = place(n)

    def dev(a, b, c, d, e):
        return {"tmpl": index_of(a, b, c, d, e)}

    near = [(b, d) for b in range(2) for d in range(2) if b or d]
    far = [(a, c, e) for a in range(highs) for c in range(2) for e in range(2) if a or c or e]

    def flip(bit, by):
        return 1 - bit if by else bit

    near_at = [(flip(low, b), flip(x, d)) for b, d in near]
    near_to = [dev(high, b, y, d, core) for b, d in near_at]
    far_to = [dev(lax.rem(high + a, highs), low, flip(y, c), x, flip(core, e)) for a, c, e in far]
    far_at = [(lax.rem(high + highs - a, highs), flip(y, c), flip(core, e)) for a, c, e in far]

    barrier = pltpu.get_barrier_semaphore()
    for peer in near_to + far_to:
        pl.semaphore_signal(barrier, inc=1, device_id=peer, device_id_type=pl.DeviceIdType.MESH)
    pl.semaphore_wait(barrier, len(near_to + far_to))

    def send(src, dst, s_sem, r_sem, peer):
        return pltpu.make_async_remote_copy(
            src_ref=src, dst_ref=dst, send_sem=s_sem, recv_sem=r_sem,
            device_id=peer, device_id_type=pl.DeviceIdType.MESH,
        )

    mine = low * 2 + x
    sent = []
    for i, peer in enumerate(near_to):
        cp = send(both_ref, held.at[mine], as_sem.at[i], ar_sem.at[i], peer)
        cp.start()
        sent.append(cp)
    held[mine] = both_ref[...]
    for i, (b, d) in enumerate(near_at):
        spot = held.at[b * 2 + d]
        send(spot, spot, as_sem.at[i], ar_sem.at[i], near_to[i]).wait_recv()
    total = (held[0] + held[1]) + (held[2] + held[3])
    picked, square = total[:, 0:1], total[:, 1:2]
    weight = (picked * picked / (square / columns + eps)).astype(jnp.bfloat16).astype(jnp.float32)
    row = lax.broadcasted_iota(jnp.int32, total.shape, 1)
    info_ref[high, y, core] = jnp.where(row == 0, weight, both_ref[...])
    own = info_ref.at[high, y, core]
    for i, peer in enumerate(far_to):
        cp = send(own, own, bs_sem.at[i], br_sem.at[i], peer)
        cp.start()
        sent.append(cp)
    for i, at in enumerate(far_at):
        spot = info_ref.at[at[0], at[1], at[2]]
        send(spot, spot, bs_sem.at[i], br_sem.at[i], far_to[i]).wait_recv()
    for cp in sent:
        cp.wait_send()


def weigh_blocks(n, columns, both):
    highs = n // 16
    return pl.pallas_call(
        functools.partial(weigh_kernel, n, columns),
        out_shape=jax.ShapeDtypeStruct((highs, 2, 2) + both.shape, jnp.float32),
        in_specs=[pl.BlockSpec(memory_space=pltpu.VMEM)],
        out_specs=pl.BlockSpec(memory_space=pltpu.VMEM),
        scratch_shapes=[
            pltpu.VMEM((4,) + both.shape, jnp.float32),
            pltpu.SemaphoreType.DMA((3,)),
            pltpu.SemaphoreType.DMA((3,)),
            pltpu.SemaphoreType.DMA((4 * highs - 1,)),
            pltpu.SemaphoreType.DMA((4 * highs - 1,)),
        ],
        compiler_params=pltpu.CompilerParams(collective_id=1, has_side_effects=True),
        cost_estimate=pl.CostEstimate(flops=0, bytes_accessed=20000000, transcendentals=0),
    )(both)


def sum_kernel(n, mix_ref, least_ref, parts_ref, sibs_ref, out_ref, buf, y_out, y_in, kept, h_out, h_in,
               buf_sem, ys_sem, yr_sem, hs_sem, hr_sem):
    highs = n // 16
    high, low, y, x, core = place(n)
    bins = out_ref.shape[0]
    span = highs * bins
    rows = parts_ref.shape[0]
    steps = out_ref.shape[1] // WIDTH

    def dev(a, c):
        return {"tmpl": index_of(a, low, c, x, core)}

    to_y = dev(high, 1 - y)
    to_high = [dev(lax.rem(high + k, highs), y) for k in range(1, highs)]

    barrier = pltpu.get_barrier_semaphore()
    for peer in [to_y] + to_high:
        pl.semaphore_signal(barrier, inc=1, device_id=peer, device_id_type=pl.DeviceIdType.MESH)
    pl.semaphore_wait(barrier, highs)

    def load(j, slot):
        at = pl.ds(pl.multiple_of(j * WIDTH, WIDTH), WIDTH)
        return (
            pltpu.make_async_copy(parts_ref.at[:, at], buf.at[slot, 0], buf_sem.at[slot, 0]),
            pltpu.make_async_copy(sibs_ref.at[:, at], buf.at[slot, 1], buf_sem.at[slot, 1]),
        )

    def send_y(j):
        return pltpu.make_async_remote_copy(
            src_ref=y_out.at[j], dst_ref=y_in.at[j], send_sem=ys_sem.at[j], recv_sem=yr_sem.at[j],
            device_id=to_y, device_id_type=pl.DeviceIdType.MESH,
        )

    def send_h(j, k):
        return pltpu.make_async_remote_copy(
            src_ref=h_out.at[j, k - 1], dst_ref=h_in.at[j, k - 1],
            send_sem=hs_sem.at[j, k - 1], recv_sem=hr_sem.at[j, k - 1],
            device_id=to_high[k - 1], device_id_type=pl.DeviceIdType.MESH,
        )

    for cp in load(0, 0):
        cp.start()

    def form(j, carry):
        slot = lax.rem(j, 2)

        @pl.when(j + 1 < steps)
        def _():
            for cp in load(j + 1, 1 - slot):
                cp.start()

        for cp in load(j, slot):
            cp.wait()
        mix = mix_ref[...]
        both = jnp.dot(mix[:, :rows], buf[slot, 0], preferred_element_type=jnp.float32)
        both += jnp.dot(mix[:, rows:], buf[slot, 1], preferred_element_type=jnp.float32)
        y_out[j] = both[:span].astype(jnp.bfloat16)
        kept[j] = both[span:]
        send_y(j).start()
        return carry

    def merge(j, carry):
        send_y(j).wait_recv()
        total = kept[j] + y_in[j].astype(jnp.float32)
        kept[j] = total
        for k in range(1, highs):
            h_out[j, k - 1] = total[k * bins:(k + 1) * bins].astype(jnp.bfloat16)
            send_h(j, k).start()
        return carry

    def finish(j, carry):
        total = kept[j][:bins]
        for k in range(1, highs):
            send_h(j, k).wait_recv()
            total += h_in[j, k - 1].astype(jnp.float32)
        out_ref[:, pl.ds(pl.multiple_of(j * WIDTH, WIDTH), WIDTH)] = total / least_ref[:, 0:1]
        return carry

    def drain(j, carry):
        send_y(j).wait_send()
        for k in range(1, highs):
            send_h(j, k).wait_send()
        return carry

    for stage in (form, merge, finish, drain):
        lax.fori_loop(0, steps, stage, 0)


def sum_blocks(n, mix, least, parts, sibs):
    highs = n // 16
    rows, pix = parts.shape
    bins = least.shape[0]
    steps = pix // WIDTH
    anywhere = pl.BlockSpec(memory_space=pl.ANY)
    local = pl.BlockSpec(memory_space=pltpu.VMEM)
    return pl.pallas_call(
        functools.partial(sum_kernel, n),
        out_shape=jax.ShapeDtypeStruct((bins, pix), jnp.float32),
        in_specs=[local, local, anywhere, anywhere],
        out_specs=local,
        scratch_shapes=[
            pltpu.VMEM((2, 2, rows, WIDTH), jnp.bfloat16),
            pltpu.VMEM((steps, highs * bins, WIDTH), jnp.bfloat16),
            pltpu.VMEM((steps, highs * bins, WIDTH), jnp.bfloat16),
            pltpu.VMEM((steps, highs * bins, WIDTH), jnp.float32),
            pltpu.VMEM((steps, highs - 1, bins, WIDTH), jnp.bfloat16),
            pltpu.VMEM((steps, highs - 1, bins, WIDTH), jnp.bfloat16),
            pltpu.SemaphoreType.DMA((2, 2)),
            pltpu.SemaphoreType.DMA((steps,)),
            pltpu.SemaphoreType.DMA((steps,)),
            pltpu.SemaphoreType.DMA((steps, highs - 1)),
            pltpu.SemaphoreType.DMA((steps, highs - 1)),
        ],
        compiler_params=pltpu.CompilerParams(
            collective_id=2, has_side_effects=True, vmem_limit_bytes=48 * 1024 * 1024
        ),
        cost_estimate=pl.CostEstimate(
            flops=4 * rows * mix.shape[0] * pix, bytes_accessed=4 * rows * pix, transcendentals=0
        ),
    )(mix, least, parts, sibs)


def body(particles, templates, classes, rotations):
    rows, pix = particles.shape
    local_classes, rot_count, _ = templates.shape
    n = lax.axis_size("tmpl")
    highs = n // 16
    bins = local_classes * rot_count
    total_bins = bins * n
    high, low, y, x, core = place(n)
    me = lax.axis_index("tmpl")

    class_ids = classes[:, 0]
    target = class_ids // local_classes * bins + rotations * local_classes + class_ids % local_classes
    label = jnp.pad(target[None], ((2, 5), (0, 0)))
    flat = templates.transpose(1, 0, 2).reshape(bins, pix)
    parts, sibs, _, labels, scores = gather_blocks(n, particles, flat, label)
    parts = parts.reshape(4 * rows, pix)
    sibs = sibs.reshape(4 * rows, pix)
    if lax.axis_size("dom") > 1:
        scores = lax.psum(scores, "dom")

    shape = (highs, 2, 2, bins)
    owner, o_y, o_c, o_b = [lax.broadcasted_iota(jnp.int32, shape, i) for i in range(4)]
    column = (index_of(owner, low, o_y, x, o_c) * bins + o_b).reshape(1, 4 * highs * bins)
    near = labels[:, 2].reshape(4 * rows)
    picked = jnp.sum(jnp.where(column == near[:, None], scores, 0.0), axis=1)
    square = jnp.sum(scores * scores, axis=1)
    both = jnp.stack([picked.reshape(4, rows), square.reshape(4, rows)], axis=1)
    both = jnp.pad(both, ((0, 0), (0, 6), (0, 0))) + labels.astype(jnp.float32)
    info = weigh_blocks(n, float(total_bins), both)

    def rows_of(e):
        block = lax.dynamic_slice(info, (high, y, e, 0, 0, 0), (1, 1, 1, 4, 8, rows))
        return block.reshape(4, 8, rows)

    here = rows_of(core)
    weights = lax.dynamic_index_in_dim(here, low * 2 + x, 0, keepdims=False)[0].astype(jnp.bfloat16)
    chip = jnp.stack([here, rows_of(1 - core)])
    chip_w = chip[:, :, 0].reshape(1, 8 * rows)
    chip_t = chip[:, :, 2].astype(jnp.int32).reshape(1, 8 * rows)
    shape = (2, highs, bins)
    flip, ahead, o_b = [lax.broadcasted_iota(jnp.int32, shape, i) for i in range(3)]
    o_y = jnp.where(flip == 0, 1 - y, y)
    wanted = index_of((high + ahead) % highs, low, o_y, x, core) * bins + o_b
    mix = jnp.where(wanted.reshape(2 * highs * bins, 1) == chip_t, chip_w, 0.0).astype(jnp.bfloat16)

    all_w = info[..., 0, :].reshape(1, n * rows)
    all_t = info[..., 2, :].astype(jnp.int32).reshape(1, n * rows)
    own = me * bins + lax.broadcasted_iota(jnp.int32, (bins, 1), 0)
    totals = jnp.sum(jnp.where(own == all_t, all_w, 0.0), axis=1)
    least = jnp.broadcast_to(jnp.maximum(totals, 1.0)[:, None], (bins, 128))
    means = sum_blocks(n, mix, least, parts, sibs)
    return means.reshape(rot_count, local_classes, pix).transpose(1, 0, 2), weights


def solution(mesh):
    return jax.shard_map(
        body,
        mesh=mesh,
        in_specs=(P("tmpl", "dom"), P("tmpl", None, "dom"), P("tmpl", None), P("tmpl")),
        out_specs=(P("tmpl", None, "dom"), P("tmpl")),
        check_vma=False,
    )
```

```python
import functools

import jax
import jax.numpy as jnp
from jax import lax
from jax.experimental import pallas as pl
from jax.experimental.pallas import tpu as pltpu
from jax.sharding import PartitionSpec as P

CHUNKS = 4
VIA_SPAN = 1
WIDTH = 1024

eps = 1e-05


def place(n):
    me = lax.axis_index("tmpl")
    core = lax.rem(me, 2)
    x = lax.rem(me // 2, 2)
    y = lax.rem(me // 4, 2)
    low = lax.rem(me // 8, 2)
    high = me // 16
    return high, low, y, x, core


def index_of(high, low, y, x, core):
    return (((high * 2 + low) * 2 + y) * 2 + x) * 2 + core


def gather_kernel(n, part_ref, temp_ref, label_ref, parts_ref, sibs_ref, temps_ref, labels_ref, score_ref, p_buf, t_buf, buf_sem, own_sem, ps_sem, pr_sem, ts_sem, tr_sem, ls_sem, lr_sem):
    highs = n // 16
    high, low, y, x, core = place(n)
    pix = part_ref.shape[1]
    width = pix // CHUNKS

    def dev(a, b, c, d, e):
        return {"tmpl": index_of(a, b, c, d, e)}

    to_low = dev(high, 1 - low, y, x, core)
    to_x = dev(high, low, y, 1 - x, core)
    to_diag = dev(high, 1 - low, y, 1 - x, core)
    to_y = dev(high, low, 1 - y, x, core)
    to_core = dev(high, low, y, x, 1 - core)
    others = [lax.rem(high + step, highs) for step in range(1, highs)]
    to_high = [dev(o, low, y, x, core) for o in others]
    came_high = [lax.rem(high + highs - step, highs) for step in range(1, highs)]

    barrier = pltpu.get_barrier_semaphore()
    peers = [to_low, to_x, to_diag, to_y, to_core] + to_high
    for peer in peers:
        pl.semaphore_signal(barrier, inc=1, device_id=peer, device_id_type=pl.DeviceIdType.MESH)
    pl.semaphore_wait(barrier, len(peers))

    def cols(j):
        return pl.ds(j * width, width)

    def send(src, dst, s_sem, r_sem, peer):
        return pltpu.make_async_remote_copy(
            src_ref=src, dst_ref=dst, send_sem=s_sem, recv_sem=r_sem,
            device_id=peer, device_id_type=pl.DeviceIdType.MESH,
        )

    def part(b, d, j):
        return parts_ref.at[b, d, :, cols(j)]

    def temp(a, c, e, j):
        return temps_ref.at[a, c, e, :, cols(j)]

    y0 = highs - 1
    c0 = y0 + highs
    sent = []

    def t_send(kind, src, slot, j, peer):
        cp = send(src, temp(*slot, j), ts_sem.at[kind, j], tr_sem.at[kind, j], peer)
        cp.start()
        sent.append(cp)

    def t_wait(kind, slot, j, peer):
        send(temp(*slot, j), temp(*slot, j), ts_sem.at[kind, j], tr_sem.at[kind, j], peer).wait_recv()

    def p_send(kind, src, slot, j, peer):
        cp = send(src, part(*slot, j), ps_sem.at[kind, j], pr_sem.at[kind, j], peer)
        cp.start()
        sent.append(cp)

    def p_share(i, src, slot, j):
        there = sibs_ref.at[slot[0], slot[1], :, cols(j)]
        cp = send(src, there, ps_sem.at[3 + i, j], pr_sem.at[3 + i, j], to_core)
        cp.start()
        sent.append(cp)

    def p_wait(kind, slot, j, peer):
        send(part(*slot, j), part(*slot, j), ps_sem.at[kind, j], pr_sem.at[kind, j], peer).wait_recv()

    spot = labels_ref.at[low * 2 + x]
    for i, peer in enumerate((to_low, to_x, to_diag)):
        cp = send(label_ref, spot, ls_sem.at[i], lr_sem.at[i], peer)
        cp.start()
        sent.append(cp)
    for j in range(CHUNKS):
        own_t = temp_ref.at[:, cols(j)]
        own_p = part_ref.at[:, cols(j)]
        for i in range(highs - 1):
            t_send(i, own_t, (high, y, core), j, to_high[i])
        k = (j + VIA_SPAN) % CHUNKS
        p_send(0, part_ref.at[:, cols(k)], (low, x), k, to_low)
        p_send(1, own_p, (low, x), j, to_x)
        p_share(0, own_p, (low, x), j)
        t_send(y0, own_t, (high, y, core), j, to_y)
        t_send(c0, own_t, (high, y, core), j, to_core)
    own = [
        pltpu.make_async_copy(part_ref, parts_ref.at[low, x], own_sem.at[0]),
        pltpu.make_async_copy(temp_ref, temps_ref.at[high, y, core], own_sem.at[1]),
        pltpu.make_async_copy(label_ref, spot, own_sem.at[2]),
    ]
    for cp in own:
        cp.start()

    def first_hop(j):
        for i in range(highs - 1):
            slot = (came_high[i], y, core)
            t_wait(i, slot, j, to_high[i])
            t_send(y0 + 1 + i, temp(*slot, j), slot, j, to_y)
            t_send(c0 + 1 + i, temp(*slot, j), slot, j, to_core)
        k = (j + VIA_SPAN) % CHUNKS
        p_wait(0, (1 - low, x), k, to_low)
        if k >= VIA_SPAN:
            p_send(2, part(1 - low, x, k), (1 - low, x), k, to_x)
        p_share(1, part(1 - low, x, k), (1 - low, x), k)
        p_wait(1, (low, 1 - x), j, to_x)
        if j < VIA_SPAN:
            p_send(2, part(low, 1 - x, j), (low, 1 - x), j, to_low)
        p_share(2, part(low, 1 - x, j), (low, 1 - x), j)
        slot = (high, 1 - y, core)
        t_wait(y0, slot, j, to_y)
        t_send(c0 + highs, temp(*slot, j), slot, j, to_core)

    def second_hop(j):
        for i in range(highs - 1):
            slot = (came_high[i], 1 - y, core)
            t_wait(y0 + 1 + i, slot, j, to_y)
            t_send(c0 + highs + 1 + i, temp(*slot, j), slot, j, to_core)

    def diagonal(j):
        p_wait(2, (1 - low, 1 - x), j, to_low if j < VIA_SPAN else to_x)
        p_share(3, part(1 - low, 1 - x, j), (1 - low, 1 - x), j)

    def loads(j):
        return (
            pltpu.make_async_copy(parts_ref.at[:, :, :, cols(j)], p_buf.at[order.index(j) % 2], buf_sem.at[order.index(j) % 2, 0]),
            pltpu.make_async_copy(temps_ref.at[:, :, :, :, cols(j)], t_buf.at[order.index(j) % 2], buf_sem.at[order.index(j) % 2, 1]),
        )

    def third_hop(j):
        for half in range(2):
            row = y if half == 0 else 1 - y
            t_wait(c0 + half * highs, (high, row, 1 - core), j, to_core)
            for i in range(highs - 1):
                t_wait(c0 + half * highs + 1 + i, (came_high[i], row, 1 - core), j, to_core)
        for cp in loads(j):
            cp.start()

    def score(j):
        for cp in loads(j):
            cp.wait()
        left = p_buf[order.index(j) % 2].reshape(4 * part_ref.shape[0], width)
        slots = [(a, c, e) for a in range(highs) for c in range(2) for e in range(2)]
        right = jnp.concatenate([t_buf[(order.index(j) % 2,) + at] for at in slots], axis=0)
        more = lax.dot_general(left, right, (((1,), (1,)), ((), ())), preferred_element_type=jnp.float32)
        if j == order[0]:
            score_ref[...] = more
        else:
            score_ref[...] += more

    order = [(j + VIA_SPAN) % CHUNKS for j in range(CHUNKS)]
    for j in range(CHUNKS):
        first_hop(j)
    for j in range(CHUNKS):
        second_hop(j)
    own[0].wait()
    own[1].wait()
    for step, j in enumerate(order):
        diagonal(j)
        third_hop(j)
        if step:
            score(order[step - 1])
    score(order[-1])
    for i, at in enumerate(((low, x), (1 - low, x), (low, 1 - x), (1 - low, 1 - x))):
        for j in range(CHUNKS):
            there = sibs_ref.at[at[0], at[1], :, cols(j)]
            send(there, there, ps_sem.at[3 + i, j], pr_sem.at[3 + i, j], to_core).wait_recv()
    for i, (b, d) in enumerate(((1 - low, x), (low, 1 - x), (1 - low, 1 - x))):
        there = labels_ref.at[b * 2 + d]
        send(there, there, ls_sem.at[i], lr_sem.at[i], to_low).wait_recv()
    own[2].wait()
    for cp in sent:
        cp.wait_send()


def gather_blocks(n, particles, flat_templates, label):
    highs = n // 16
    rows, pix = particles.shape
    bins = flat_templates.shape[0]
    kinds = 3 * highs - 1 + highs
    total = (rows * 4 + bins * 4 * highs) * pix * 2
    return pl.pallas_call(
        functools.partial(gather_kernel, n),
        out_shape=(
            jax.ShapeDtypeStruct((2, 2, rows, pix), jnp.bfloat16),
            jax.ShapeDtypeStruct((2, 2, rows, pix), jnp.bfloat16),
            jax.ShapeDtypeStruct((highs, 2, 2, bins, pix), jnp.bfloat16),
            jax.ShapeDtypeStruct((4,) + label.shape, label.dtype),
            jax.ShapeDtypeStruct((4 * rows, 4 * highs * bins), jnp.float32),
        ),
        in_specs=[pl.BlockSpec(memory_space=pl.ANY)] * 3,
        out_specs=[pl.BlockSpec(memory_space=pl.ANY)] * 4 + [pl.BlockSpec(memory_space=pltpu.VMEM)],
        scratch_shapes=[
            pltpu.VMEM((2, 2, 2, rows, pix // CHUNKS), jnp.bfloat16),
            pltpu.VMEM((2, highs, 2, 2, bins, pix // CHUNKS), jnp.bfloat16),
            pltpu.SemaphoreType.DMA((2, 2)),
            pltpu.SemaphoreType.DMA((3,)),
            pltpu.SemaphoreType.DMA((7, CHUNKS)),
            pltpu.SemaphoreType.DMA((7, CHUNKS)),
            pltpu.SemaphoreType.DMA((kinds, CHUNKS)),
            pltpu.SemaphoreType.DMA((kinds, CHUNKS)),
            pltpu.SemaphoreType.DMA((3,)),
            pltpu.SemaphoreType.DMA((3,)),
        ],
        compiler_params=pltpu.CompilerParams(
            collective_id=0, has_side_effects=True, vmem_limit_bytes=48 * 1024 * 1024
        ),
        cost_estimate=pl.CostEstimate(flops=0, bytes_accessed=10 * total, transcendentals=0),
    )(particles, flat_templates, label)


def weigh_kernel(n, columns, both_ref, info_ref, held, as_sem, ar_sem, bs_sem, br_sem):
    highs = n // 16
    high, low, y, x, core = place(n)

    def dev(a, b, c, d, e):
        return {"tmpl": index_of(a, b, c, d, e)}

    near = [(b, d) for b in range(2) for d in range(2) if b or d]
    far = [(a, c, e) for a in range(highs) for c in range(2) for e in range(2) if a or c or e]

    def flip(bit, by):
        return 1 - bit if by else bit

    near_at = [(flip(low, b), flip(x, d)) for b, d in near]
    near_to = [dev(high, b, y, d, core) for b, d in near_at]
    far_to = [dev(lax.rem(high + a, highs), low, flip(y, c), x, flip(core, e)) for a, c, e in far]
    far_at = [(lax.rem(high + highs - a, highs), flip(y, c), flip(core, e)) for a, c, e in far]

    barrier = pltpu.get_barrier_semaphore()
    for peer in near_to + far_to:
        pl.semaphore_signal(barrier, inc=1, device_id=peer, device_id_type=pl.DeviceIdType.MESH)
    pl.semaphore_wait(barrier, len(near_to + far_to))

    def send(src, dst, s_sem, r_sem, peer):
        return pltpu.make_async_remote_copy(
            src_ref=src, dst_ref=dst, send_sem=s_sem, recv_sem=r_sem,
            device_id=peer, device_id_type=pl.DeviceIdType.MESH,
        )

    mine = low * 2 + x
    sent = []
    for i, peer in enumerate(near_to):
        cp = send(both_ref, held.at[mine], as_sem.at[i], ar_sem.at[i], peer)
        cp.start()
        sent.append(cp)
    held[mine] = both_ref[...]
    for i, (b, d) in enumerate(near_at):
        spot = held.at[b * 2 + d]
        send(spot, spot, as_sem.at[i], ar_sem.at[i], near_to[i]).wait_recv()
    total = (held[0] + held[1]) + (held[2] + held[3])
    picked, square = total[:, 0:1], total[:, 1:2]
    weight = (picked * picked / (square / columns + eps)).astype(jnp.bfloat16).astype(jnp.float32)
    row = lax.broadcasted_iota(jnp.int32, total.shape, 1)
    info_ref[high, y, core] = jnp.where(row == 0, weight, both_ref[...])
    own = info_ref.at[high, y, core]
    for i, peer in enumerate(far_to):
        cp = send(own, own, bs_sem.at[i], br_sem.at[i], peer)
        cp.start()
        sent.append(cp)
    for i, at in enumerate(far_at):
        spot = info_ref.at[at[0], at[1], at[2]]
        send(spot, spot, bs_sem.at[i], br_sem.at[i], far_to[i]).wait_recv()
    for cp in sent:
        cp.wait_send()


def weigh_blocks(n, columns, both):
    highs = n // 16
    return pl.pallas_call(
        functools.partial(weigh_kernel, n, columns),
        out_shape=jax.ShapeDtypeStruct((highs, 2, 2) + both.shape, jnp.float32),
        in_specs=[pl.BlockSpec(memory_space=pltpu.VMEM)],
        out_specs=pl.BlockSpec(memory_space=pltpu.VMEM),
        scratch_shapes=[
            pltpu.VMEM((4,) + both.shape, jnp.float32),
            pltpu.SemaphoreType.DMA((3,)),
            pltpu.SemaphoreType.DMA((3,)),
            pltpu.SemaphoreType.DMA((4 * highs - 1,)),
            pltpu.SemaphoreType.DMA((4 * highs - 1,)),
        ],
        compiler_params=pltpu.CompilerParams(collective_id=1, has_side_effects=True),
        cost_estimate=pl.CostEstimate(flops=0, bytes_accessed=20000000, transcendentals=0),
    )(both)


def sum_kernel(n, mix_ref, least_ref, parts_ref, sibs_ref, out_ref, buf, y_out, y_in, kept, h_out, h_in,
               buf_sem, ys_sem, yr_sem, hs_sem, hr_sem):
    highs = n // 16
    high, low, y, x, core = place(n)
    rots, owned, pix = out_ref.shape
    bins = rots * owned
    span = highs * bins
    rows = parts_ref.shape[0]
    steps = pix // WIDTH

    def dev(a, c):
        return {"tmpl": index_of(a, low, c, x, core)}

    to_y = dev(high, 1 - y)
    to_high = [dev(lax.rem(high + k, highs), y) for k in range(1, highs)]

    barrier = pltpu.get_barrier_semaphore()
    for peer in [to_y] + to_high:
        pl.semaphore_signal(barrier, inc=1, device_id=peer, device_id_type=pl.DeviceIdType.MESH)
    pl.semaphore_wait(barrier, highs)

    def load(j, slot):
        at = pl.ds(pl.multiple_of(j * WIDTH, WIDTH), WIDTH)
        return (
            pltpu.make_async_copy(parts_ref.at[:, at], buf.at[slot, 0], buf_sem.at[slot, 0]),
            pltpu.make_async_copy(sibs_ref.at[:, at], buf.at[slot, 1], buf_sem.at[slot, 1]),
        )

    def send_y(j):
        return pltpu.make_async_remote_copy(
            src_ref=y_out.at[j], dst_ref=y_in.at[j], send_sem=ys_sem.at[j], recv_sem=yr_sem.at[j],
            device_id=to_y, device_id_type=pl.DeviceIdType.MESH,
        )

    def send_h(j, k):
        return pltpu.make_async_remote_copy(
            src_ref=h_out.at[j, k - 1], dst_ref=h_in.at[j, k - 1],
            send_sem=hs_sem.at[j, k - 1], recv_sem=hr_sem.at[j, k - 1],
            device_id=to_high[k - 1], device_id_type=pl.DeviceIdType.MESH,
        )

    for cp in load(0, 0):
        cp.start()

    def form(j, carry):
        slot = lax.rem(j, 2)

        @pl.when(j + 1 < steps)
        def _():
            for cp in load(j + 1, 1 - slot):
                cp.start()

        for cp in load(j, slot):
            cp.wait()
        mix = mix_ref[...]
        both = jnp.dot(mix[:, :rows], buf[slot, 0], preferred_element_type=jnp.float32)
        both += jnp.dot(mix[:, rows:], buf[slot, 1], preferred_element_type=jnp.float32)
        y_out[j] = both[:span].astype(jnp.bfloat16)
        kept[j] = both[span:]
        send_y(j).start()
        return carry

    def merge(j, carry):
        send_y(j).wait_recv()
        total = kept[j] + y_in[j].astype(jnp.float32)
        kept[j] = total
        for k in range(1, highs):
            h_out[j, k - 1] = total[k * bins:(k + 1) * bins].astype(jnp.bfloat16)
            send_h(j, k).start()
        return carry

    def finish(j, carry):
        total = kept[j][:bins]
        for k in range(1, highs):
            send_h(j, k).wait_recv()
            total += h_in[j, k - 1].astype(jnp.float32)
        means = total / least_ref[:, 0:1]
        at = pl.ds(pl.multiple_of(j * WIDTH, WIDTH), WIDTH)
        for r in range(rots):
            out_ref[r, :, at] = means[r * owned:(r + 1) * owned]
        return carry

    def drain(j, carry):
        send_y(j).wait_send()
        for k in range(1, highs):
            send_h(j, k).wait_send()
        return carry

    for stage in (form, merge, finish, drain):
        lax.fori_loop(0, steps, stage, 0)


def sum_blocks(n, rots, mix, least, parts, sibs):
    highs = n // 16
    rows, pix = parts.shape
    bins = least.shape[0]
    steps = pix // WIDTH
    anywhere = pl.BlockSpec(memory_space=pl.ANY)
    local = pl.BlockSpec(memory_space=pltpu.VMEM)
    return pl.pallas_call(
        functools.partial(sum_kernel, n),
        out_shape=jax.ShapeDtypeStruct((rots, bins // rots, pix), jnp.float32),
        in_specs=[local, local, anywhere, anywhere],
        out_specs=local,
        scratch_shapes=[
            pltpu.VMEM((2, 2, rows, WIDTH), jnp.bfloat16),
            pltpu.VMEM((steps, highs * bins, WIDTH), jnp.bfloat16),
            pltpu.VMEM((steps, highs * bins, WIDTH), jnp.bfloat16),
            pltpu.VMEM((steps, highs * bins, WIDTH), jnp.float32),
            pltpu.VMEM((steps, highs - 1, bins, WIDTH), jnp.bfloat16),
            pltpu.VMEM((steps, highs - 1, bins, WIDTH), jnp.bfloat16),
            pltpu.SemaphoreType.DMA((2, 2)),
            pltpu.SemaphoreType.DMA((steps,)),
            pltpu.SemaphoreType.DMA((steps,)),
            pltpu.SemaphoreType.DMA((steps, highs - 1)),
            pltpu.SemaphoreType.DMA((steps, highs - 1)),
        ],
        compiler_params=pltpu.CompilerParams(
            collective_id=2, has_side_effects=True, vmem_limit_bytes=48 * 1024 * 1024
        ),
        cost_estimate=pl.CostEstimate(
            flops=4 * rows * mix.shape[0] * pix, bytes_accessed=4 * rows * pix, transcendentals=0
        ),
    )(mix, least, parts, sibs)


def body(particles, templates, classes, rotations):
    rows, pix = particles.shape
    local_classes, rot_count, _ = templates.shape
    n = lax.axis_size("tmpl")
    highs = n // 16
    bins = local_classes * rot_count
    total_bins = bins * n
    high, low, y, x, core = place(n)
    me = lax.axis_index("tmpl")

    class_ids = classes[:, 0]
    target = class_ids // local_classes * bins + rotations * local_classes + class_ids % local_classes
    label = jnp.pad(target[None], ((2, 5), (0, 0)))
    flat = templates.transpose(1, 0, 2).reshape(bins, pix)
    parts, sibs, _, labels, scores = gather_blocks(n, particles, flat, label)
    parts = parts.reshape(4 * rows, pix)
    sibs = sibs.reshape(4 * rows, pix)
    if lax.axis_size("dom") > 1:
        scores = lax.psum(scores, "dom")

    shape = (highs, 2, 2, bins)
    owner, o_y, o_c, o_b = [lax.broadcasted_iota(jnp.int32, shape, i) for i in range(4)]
    column = (index_of(owner, low, o_y, x, o_c) * bins + o_b).reshape(1, 4 * highs * bins)
    near = labels[:, 2].reshape(4 * rows)
    picked = jnp.sum(jnp.where(column == near[:, None], scores, 0.0), axis=1)
    square = jnp.sum(scores * scores, axis=1)
    both = jnp.stack([picked.reshape(4, rows), square.reshape(4, rows)], axis=1)
    both = jnp.pad(both, ((0, 0), (0, 6), (0, 0))) + labels.astype(jnp.float32)
    info = weigh_blocks(n, float(total_bins), both)

    def rows_of(e):
        block = lax.dynamic_slice(info, (high, y, e, 0, 0, 0), (1, 1, 1, 4, 8, rows))
        return block.reshape(4, 8, rows)

    here = rows_of(core)
    weights = lax.dynamic_index_in_dim(here, low * 2 + x, 0, keepdims=False)[0].astype(jnp.bfloat16)
    chip = jnp.stack([here, rows_of(1 - core)])
    chip_w = chip[:, :, 0].reshape(1, 8 * rows)
    chip_t = chip[:, :, 2].astype(jnp.int32).reshape(1, 8 * rows)
    shape = (2, highs, bins)
    flip, ahead, o_b = [lax.broadcasted_iota(jnp.int32, shape, i) for i in range(3)]
    o_y = jnp.where(flip == 0, 1 - y, y)
    wanted = index_of((high + ahead) % highs, low, o_y, x, core) * bins + o_b
    mix = jnp.where(wanted.reshape(2 * highs * bins, 1) == chip_t, chip_w, 0.0).astype(jnp.bfloat16)

    all_w = info[..., 0, :].reshape(1, n * rows)
    all_t = info[..., 2, :].astype(jnp.int32).reshape(1, n * rows)
    own = me * bins + lax.broadcasted_iota(jnp.int32, (bins, 1), 0)
    totals = jnp.sum(jnp.where(own == all_t, all_w, 0.0), axis=1)
    least = jnp.broadcast_to(jnp.maximum(totals, 1.0)[:, None], (bins, 128))
    means = sum_blocks(n, rot_count, mix, least, parts, sibs)
    return means.transpose(1, 0, 2), weights


def solution(mesh):
    return jax.shard_map(
        body,
        mesh=mesh,
        in_specs=(P("tmpl", "dom"), P("tmpl", None, "dom"), P("tmpl", None), P("tmpl")),
        out_specs=(P("tmpl", None, "dom"), P("tmpl")),
        check_vma=False,
    )
```

```python
import functools

import jax
import jax.numpy as jnp
from jax import lax
from jax.experimental import pallas as pl
from jax.experimental.pallas import tpu as pltpu
from jax.sharding import PartitionSpec as P

CHUNKS = 4
VIA_SPAN = 1
WIDTH = 1024

eps = 1e-05


def place(n):
    me = lax.axis_index("tmpl")
    core = lax.rem(me, 2)
    x = lax.rem(me // 2, 2)
    y = lax.rem(me // 4, 2)
    low = lax.rem(me // 8, 2)
    high = me // 16
    return high, low, y, x, core


def index_of(high, low, y, x, core):
    return (((high * 2 + low) * 2 + y) * 2 + x) * 2 + core


def gather_kernel(n, part_ref, temp_ref, label_ref, parts_ref, sibs_ref, temps_ref, labels_ref, score_ref, p_buf, t_buf, buf_sem, own_sem, ps_sem, pr_sem, ts_sem, tr_sem, ls_sem, lr_sem):
    highs = n // 16
    high, low, y, x, core = place(n)
    pix = part_ref.shape[1]
    width = pix // CHUNKS

    def dev(a, b, c, d, e):
        return {"tmpl": index_of(a, b, c, d, e)}

    to_low = dev(high, 1 - low, y, x, core)
    to_x = dev(high, low, y, 1 - x, core)
    to_diag = dev(high, 1 - low, y, 1 - x, core)
    to_y = dev(high, low, 1 - y, x, core)
    to_core = dev(high, low, y, x, 1 - core)
    others = [lax.rem(high + step, highs) for step in range(1, highs)]
    to_high = [dev(o, low, y, x, core) for o in others]
    came_high = [lax.rem(high + highs - step, highs) for step in range(1, highs)]

    barrier = pltpu.get_barrier_semaphore()
    peers = [to_low, to_x, to_diag, to_y, to_core] + to_high
    for peer in peers:
        pl.semaphore_signal(barrier, inc=1, device_id=peer, device_id_type=pl.DeviceIdType.MESH)
    pl.semaphore_wait(barrier, len(peers))

    def cols(j):
        return pl.ds(j * width, width)

    def send(src, dst, s_sem, r_sem, peer):
        return pltpu.make_async_remote_copy(
            src_ref=src, dst_ref=dst, send_sem=s_sem, recv_sem=r_sem,
            device_id=peer, device_id_type=pl.DeviceIdType.MESH,
        )

    def part(b, d, j):
        return parts_ref.at[b, d, :, cols(j)]

    def temp(a, c, e, j):
        return temps_ref.at[a, c, e, :, cols(j)]

    y0 = highs - 1
    c0 = y0 + highs
    sent = []

    def t_send(kind, src, slot, j, peer):
        cp = send(src, temp(*slot, j), ts_sem.at[kind, j], tr_sem.at[kind, j], peer)
        cp.start()
        sent.append(cp)

    def t_wait(kind, slot, j, peer):
        send(temp(*slot, j), temp(*slot, j), ts_sem.at[kind, j], tr_sem.at[kind, j], peer).wait_recv()

    def p_send(kind, src, slot, j, peer):
        cp = send(src, part(*slot, j), ps_sem.at[kind, j], pr_sem.at[kind, j], peer)
        cp.start()
        sent.append(cp)

    def p_share(i, src, slot, j):
        there = sibs_ref.at[slot[0], slot[1], :, cols(j)]
        cp = send(src, there, ps_sem.at[3 + i, j], pr_sem.at[3 + i, j], to_core)
        cp.start()
        sent.append(cp)

    def p_wait(kind, slot, j, peer):
        send(part(*slot, j), part(*slot, j), ps_sem.at[kind, j], pr_sem.at[kind, j], peer).wait_recv()

    spot = labels_ref.at[low * 2 + x]
    for i, peer in enumerate((to_low, to_x, to_diag)):
        cp = send(label_ref, spot, ls_sem.at[i], lr_sem.at[i], peer)
        cp.start()
        sent.append(cp)
    for j in range(CHUNKS):
        own_t = temp_ref.at[:, cols(j)]
        own_p = part_ref.at[:, cols(j)]
        for i in range(highs - 1):
            t_send(i, own_t, (high, y, core), j, to_high[i])
        k = (j + VIA_SPAN) % CHUNKS
        p_send(0, part_ref.at[:, cols(k)], (low, x), k, to_low)
        p_send(1, own_p, (low, x), j, to_x)
        p_share(0, own_p, (low, x), j)
        t_send(y0, own_t, (high, y, core), j, to_y)
        t_send(c0, own_t, (high, y, core), j, to_core)
    own = [
        pltpu.make_async_copy(part_ref, parts_ref.at[low, x], own_sem.at[0]),
        pltpu.make_async_copy(temp_ref, temps_ref.at[high, y, core], own_sem.at[1]),
        pltpu.make_async_copy(label_ref, spot, own_sem.at[2]),
    ]
    for cp in own:
        cp.start()

    def first_hop(j):
        for i in range(highs - 1):
            slot = (came_high[i], y, core)
            t_wait(i, slot, j, to_high[i])
            t_send(y0 + 1 + i, temp(*slot, j), slot, j, to_y)
            t_send(c0 + 1 + i, temp(*slot, j), slot, j, to_core)
        k = (j + VIA_SPAN) % CHUNKS
        p_wait(0, (1 - low, x), k, to_low)
        if k >= VIA_SPAN:
            p_send(2, part(1 - low, x, k), (1 - low, x), k, to_x)
        p_share(1, part(1 - low, x, k), (1 - low, x), k)
        p_wait(1, (low, 1 - x), j, to_x)
        if j < VIA_SPAN:
            p_send(2, part(low, 1 - x, j), (low, 1 - x), j, to_low)
        p_share(2, part(low, 1 - x, j), (low, 1 - x), j)
        slot = (high, 1 - y, core)
        t_wait(y0, slot, j, to_y)
        t_send(c0 + highs, temp(*slot, j), slot, j, to_core)

    def second_hop(j):
        for i in range(highs - 1):
            slot = (came_high[i], 1 - y, core)
            t_wait(y0 + 1 + i, slot, j, to_y)
            t_send(c0 + highs + 1 + i, temp(*slot, j), slot, j, to_core)

    def diagonal(j):
        p_wait(2, (1 - low, 1 - x), j, to_low if j < VIA_SPAN else to_x)
        p_share(3, part(1 - low, 1 - x, j), (1 - low, 1 - x), j)

    def loads(j):
        return (
            pltpu.make_async_copy(parts_ref.at[:, :, :, cols(j)], p_buf.at[order.index(j) % 2], buf_sem.at[order.index(j) % 2, 0]),
            pltpu.make_async_copy(temps_ref.at[:, :, :, :, cols(j)], t_buf.at[order.index(j) % 2], buf_sem.at[order.index(j) % 2, 1]),
        )

    def third_hop(j):
        for half in range(2):
            row = y if half == 0 else 1 - y
            t_wait(c0 + half * highs, (high, row, 1 - core), j, to_core)
            for i in range(highs - 1):
                t_wait(c0 + half * highs + 1 + i, (came_high[i], row, 1 - core), j, to_core)
        for cp in loads(j):
            cp.start()

    def score(j):
        for cp in loads(j):
            cp.wait()
        left = p_buf[order.index(j) % 2].reshape(4 * part_ref.shape[0], width)
        slots = [(a, c, e) for a in range(highs) for c in range(2) for e in range(2)]
        right = jnp.concatenate([t_buf[(order.index(j) % 2,) + at] for at in slots], axis=0)
        more = lax.dot_general(left, right, (((1,), (1,)), ((), ())), preferred_element_type=jnp.float32)
        if j == order[0]:
            score_ref[...] = more
        else:
            score_ref[...] += more

    order = [(j + VIA_SPAN) % CHUNKS for j in range(CHUNKS)]
    for j in range(CHUNKS):
        first_hop(j)
    for j in range(CHUNKS):
        second_hop(j)
    own[0].wait()
    own[1].wait()
    for step, j in enumerate(order):
        diagonal(j)
        third_hop(j)
        if step:
            score(order[step - 1])
    score(order[-1])
    for i, at in enumerate(((low, x), (1 - low, x), (low, 1 - x), (1 - low, 1 - x))):
        for j in range(CHUNKS):
            there = sibs_ref.at[at[0], at[1], :, cols(j)]
            send(there, there, ps_sem.at[3 + i, j], pr_sem.at[3 + i, j], to_core).wait_recv()
    for i, (b, d) in enumerate(((1 - low, x), (low, 1 - x), (1 - low, 1 - x))):
        there = labels_ref.at[b * 2 + d]
        send(there, there, ls_sem.at[i], lr_sem.at[i], to_low).wait_recv()
    own[2].wait()
    for cp in sent:
        cp.wait_send()


def gather_blocks(n, particles, flat_templates, label):
    highs = n // 16
    rows, pix = particles.shape
    bins = flat_templates.shape[0]
    kinds = 3 * highs - 1 + highs
    total = (rows * 4 + bins * 4 * highs) * pix * 2
    return pl.pallas_call(
        functools.partial(gather_kernel, n),
        out_shape=(
            jax.ShapeDtypeStruct((2, 2, rows, pix), jnp.bfloat16),
            jax.ShapeDtypeStruct((2, 2, rows, pix), jnp.bfloat16),
            jax.ShapeDtypeStruct((highs, 2, 2, bins, pix), jnp.bfloat16),
            jax.ShapeDtypeStruct((4,) + label.shape, label.dtype),
            jax.ShapeDtypeStruct((4 * rows, 4 * highs * bins), jnp.float32),
        ),
        in_specs=[pl.BlockSpec(memory_space=pl.ANY)] * 3,
        out_specs=[pl.BlockSpec(memory_space=pl.ANY)] * 4 + [pl.BlockSpec(memory_space=pltpu.VMEM)],
        scratch_shapes=[
            pltpu.VMEM((2, 2, 2, rows, pix // CHUNKS), jnp.bfloat16),
            pltpu.VMEM((2, highs, 2, 2, bins, pix // CHUNKS), jnp.bfloat16),
            pltpu.SemaphoreType.DMA((2, 2)),
            pltpu.SemaphoreType.DMA((3,)),
            pltpu.SemaphoreType.DMA((7, CHUNKS)),
            pltpu.SemaphoreType.DMA((7, CHUNKS)),
            pltpu.SemaphoreType.DMA((kinds, CHUNKS)),
            pltpu.SemaphoreType.DMA((kinds, CHUNKS)),
            pltpu.SemaphoreType.DMA((3,)),
            pltpu.SemaphoreType.DMA((3,)),
        ],
        compiler_params=pltpu.CompilerParams(
            collective_id=0, has_side_effects=True, vmem_limit_bytes=48 * 1024 * 1024
        ),
        cost_estimate=pl.CostEstimate(flops=0, bytes_accessed=10 * total, transcendentals=0),
    )(particles, flat_templates, label)


def weigh_kernel(n, columns, both_ref, info_ref, held, as_sem, ar_sem, bs_sem, br_sem):
    highs = n // 16
    high, low, y, x, core = place(n)

    def dev(a, b, c, d, e):
        return {"tmpl": index_of(a, b, c, d, e)}

    near = [(b, d) for b in range(2) for d in range(2) if b or d]
    far = [(a, c, e) for a in range(highs) for c in range(2) for e in range(2) if a or c or e]

    def flip(bit, by):
        return 1 - bit if by else bit

    near_at = [(flip(low, b), flip(x, d)) for b, d in near]
    near_to = [dev(high, b, y, d, core) for b, d in near_at]
    far_to = [dev(lax.rem(high + a, highs), low, flip(y, c), x, flip(core, e)) for a, c, e in far]
    far_at = [(lax.rem(high + highs - a, highs), flip(y, c), flip(core, e)) for a, c, e in far]

    barrier = pltpu.get_barrier_semaphore()
    for peer in near_to + far_to:
        pl.semaphore_signal(barrier, inc=1, device_id=peer, device_id_type=pl.DeviceIdType.MESH)
    pl.semaphore_wait(barrier, len(near_to + far_to))

    def send(src, dst, s_sem, r_sem, peer):
        return pltpu.make_async_remote_copy(
            src_ref=src, dst_ref=dst, send_sem=s_sem, recv_sem=r_sem,
            device_id=peer, device_id_type=pl.DeviceIdType.MESH,
        )

    mine = low * 2 + x
    sent = []
    for i, peer in enumerate(near_to):
        cp = send(both_ref, held.at[mine], as_sem.at[i], ar_sem.at[i], peer)
        cp.start()
        sent.append(cp)
    held[mine] = both_ref[...]
    for i, (b, d) in enumerate(near_at):
        spot = held.at[b * 2 + d]
        send(spot, spot, as_sem.at[i], ar_sem.at[i], near_to[i]).wait_recv()
    total = (held[0] + held[1]) + (held[2] + held[3])
    picked, square = total[:, 0:1], total[:, 1:2]
    weight = (picked * picked / (square / columns + eps)).astype(jnp.bfloat16).astype(jnp.float32)
    row = lax.broadcasted_iota(jnp.int32, total.shape, 1)
    info_ref[high, y, core] = jnp.where(row == 0, weight, both_ref[...])
    own = info_ref.at[high, y, core]
    for i, peer in enumerate(far_to):
        cp = send(own, own, bs_sem.at[i], br_sem.at[i], peer)
        cp.start()
        sent.append(cp)
    for i, at in enumerate(far_at):
        spot = info_ref.at[at[0], at[1], at[2]]
        send(spot, spot, bs_sem.at[i], br_sem.at[i], far_to[i]).wait_recv()
    for cp in sent:
        cp.wait_send()


def weigh_blocks(n, columns, both):
    highs = n // 16
    return pl.pallas_call(
        functools.partial(weigh_kernel, n, columns),
        out_shape=jax.ShapeDtypeStruct((highs, 2, 2) + both.shape, jnp.float32),
        in_specs=[pl.BlockSpec(memory_space=pltpu.VMEM)],
        out_specs=pl.BlockSpec(memory_space=pltpu.VMEM),
        scratch_shapes=[
            pltpu.VMEM((4,) + both.shape, jnp.float32),
            pltpu.SemaphoreType.DMA((3,)),
            pltpu.SemaphoreType.DMA((3,)),
            pltpu.SemaphoreType.DMA((4 * highs - 1,)),
            pltpu.SemaphoreType.DMA((4 * highs - 1,)),
        ],
        compiler_params=pltpu.CompilerParams(collective_id=1, has_side_effects=True),
        cost_estimate=pl.CostEstimate(flops=0, bytes_accessed=20000000, transcendentals=0),
    )(both)


def sum_kernel(n, mix_ref, least_ref, parts_ref, sibs_ref, out_ref, buf, y_out, y_in, kept, h_out, h_in,
               buf_sem, ys_sem, yr_sem, hs_sem, hr_sem):
    highs = n // 16
    high, low, y, x, core = place(n)
    rots, owned, pix = out_ref.shape
    bins = rots * owned
    span = highs * bins
    rows = parts_ref.shape[0]
    steps = pix // WIDTH

    def dev(a, c):
        return {"tmpl": index_of(a, low, c, x, core)}

    to_y = dev(high, 1 - y)
    to_high = [dev(lax.rem(high + k, highs), y) for k in range(1, highs)]

    barrier = pltpu.get_barrier_semaphore()
    for peer in [to_y] + to_high:
        pl.semaphore_signal(barrier, inc=1, device_id=peer, device_id_type=pl.DeviceIdType.MESH)
    pl.semaphore_wait(barrier, highs)

    def load(j, slot):
        at = pl.ds(pl.multiple_of(j * WIDTH, WIDTH), WIDTH)
        return (
            pltpu.make_async_copy(parts_ref.at[:, at], buf.at[slot, 0], buf_sem.at[slot, 0]),
            pltpu.make_async_copy(sibs_ref.at[:, at], buf.at[slot, 1], buf_sem.at[slot, 1]),
        )

    def send_y(j):
        return pltpu.make_async_remote_copy(
            src_ref=y_out.at[j], dst_ref=y_in.at[j], send_sem=ys_sem.at[j], recv_sem=yr_sem.at[j],
            device_id=to_y, device_id_type=pl.DeviceIdType.MESH,
        )

    def send_h(j, k):
        return pltpu.make_async_remote_copy(
            src_ref=h_out.at[j, k - 1], dst_ref=h_in.at[j, k - 1],
            send_sem=hs_sem.at[j, k - 1], recv_sem=hr_sem.at[j, k - 1],
            device_id=to_high[k - 1], device_id_type=pl.DeviceIdType.MESH,
        )

    for cp in load(0, 0):
        cp.start()

    def form(j, carry):
        slot = lax.rem(j, 2)

        @pl.when(j + 1 < steps)
        def _():
            for cp in load(j + 1, 1 - slot):
                cp.start()

        for cp in load(j, slot):
            cp.wait()
        mix = mix_ref[...]
        both = jnp.dot(mix[:, :rows], buf[slot, 0], preferred_element_type=jnp.float32)
        both += jnp.dot(mix[:, rows:], buf[slot, 1], preferred_element_type=jnp.float32)
        y_out[j] = both[:span].astype(jnp.bfloat16)
        kept[j] = both[span:]
        send_y(j).start()
        return carry

    def merge(j, carry):
        send_y(j).wait_recv()
        total = kept[j] + y_in[j].astype(jnp.float32)
        kept[j] = total
        for k in range(1, highs):
            h_out[j, k - 1] = total[k * bins:(k + 1) * bins].astype(jnp.bfloat16)
            send_h(j, k).start()
        return carry

    def finish(j, carry):
        total = kept[j][:bins]
        for k in range(1, highs):
            send_h(j, k).wait_recv()
            total += h_in[j, k - 1].astype(jnp.float32)
        means = total / least_ref[:, 0:1]
        at = pl.ds(pl.multiple_of(j * WIDTH, WIDTH), WIDTH)
        for r in range(rots):
            out_ref[r, :, at] = means[r * owned:(r + 1) * owned]
        return carry

    def drain(j, carry):
        send_y(j).wait_send()
        for k in range(1, highs):
            send_h(j, k).wait_send()
        return carry

    def turn(t, carry):
        for stage, late in ((form, 0), (merge, 3), (finish, 6)):
            @pl.when((t >= late) & (t < steps + late))
            def _(stage=stage, late=late):
                stage(t - late, 0)

        return carry

    lax.fori_loop(0, steps + 6, turn, 0)
    lax.fori_loop(0, steps, drain, 0)


def sum_blocks(n, rots, mix, least, parts, sibs):
    highs = n // 16
    rows, pix = parts.shape
    bins = least.shape[0]
    steps = pix // WIDTH
    anywhere = pl.BlockSpec(memory_space=pl.ANY)
    local = pl.BlockSpec(memory_space=pltpu.VMEM)
    return pl.pallas_call(
        functools.partial(sum_kernel, n),
        out_shape=jax.ShapeDtypeStruct((rots, bins // rots, pix), jnp.float32),
        in_specs=[local, local, anywhere, anywhere],
        out_specs=local,
        scratch_shapes=[
            pltpu.VMEM((2, 2, rows, WIDTH), jnp.bfloat16),
            pltpu.VMEM((steps, highs * bins, WIDTH), jnp.bfloat16),
            pltpu.VMEM((steps, highs * bins, WIDTH), jnp.bfloat16),
            pltpu.VMEM((steps, highs * bins, WIDTH), jnp.float32),
            pltpu.VMEM((steps, highs - 1, bins, WIDTH), jnp.bfloat16),
            pltpu.VMEM((steps, highs - 1, bins, WIDTH), jnp.bfloat16),
            pltpu.SemaphoreType.DMA((2, 2)),
            pltpu.SemaphoreType.DMA((steps,)),
            pltpu.SemaphoreType.DMA((steps,)),
            pltpu.SemaphoreType.DMA((steps, highs - 1)),
            pltpu.SemaphoreType.DMA((steps, highs - 1)),
        ],
        compiler_params=pltpu.CompilerParams(
            collective_id=2, has_side_effects=True, vmem_limit_bytes=48 * 1024 * 1024
        ),
        cost_estimate=pl.CostEstimate(
            flops=4 * rows * mix.shape[0] * pix, bytes_accessed=4 * rows * pix, transcendentals=0
        ),
    )(mix, least, parts, sibs)


def body(particles, templates, classes, rotations):
    rows, pix = particles.shape
    local_classes, rot_count, _ = templates.shape
    n = lax.axis_size("tmpl")
    highs = n // 16
    bins = local_classes * rot_count
    total_bins = bins * n
    high, low, y, x, core = place(n)
    me = lax.axis_index("tmpl")

    class_ids = classes[:, 0]
    target = class_ids // local_classes * bins + rotations * local_classes + class_ids % local_classes
    label = jnp.pad(target[None], ((2, 5), (0, 0)))
    flat = templates.transpose(1, 0, 2).reshape(bins, pix)
    parts, sibs, _, labels, scores = gather_blocks(n, particles, flat, label)
    parts = parts.reshape(4 * rows, pix)
    sibs = sibs.reshape(4 * rows, pix)
    if lax.axis_size("dom") > 1:
        scores = lax.psum(scores, "dom")

    shape = (highs, 2, 2, bins)
    owner, o_y, o_c, o_b = [lax.broadcasted_iota(jnp.int32, shape, i) for i in range(4)]
    column = (index_of(owner, low, o_y, x, o_c) * bins + o_b).reshape(1, 4 * highs * bins)
    near = labels[:, 2].reshape(4 * rows)
    picked = jnp.sum(jnp.where(column == near[:, None], scores, 0.0), axis=1)
    square = jnp.sum(scores * scores, axis=1)
    both = jnp.stack([picked.reshape(4, rows), square.reshape(4, rows)], axis=1)
    both = jnp.pad(both, ((0, 0), (0, 6), (0, 0))) + labels.astype(jnp.float32)
    info = weigh_blocks(n, float(total_bins), both)

    def rows_of(e):
        block = lax.dynamic_slice(info, (high, y, e, 0, 0, 0), (1, 1, 1, 4, 8, rows))
        return block.reshape(4, 8, rows)

    here = rows_of(core)
    weights = lax.dynamic_index_in_dim(here, low * 2 + x, 0, keepdims=False)[0].astype(jnp.bfloat16)
    chip = jnp.stack([here, rows_of(1 - core)])
    chip_w = chip[:, :, 0].reshape(1, 8 * rows)
    chip_t = chip[:, :, 2].astype(jnp.int32).reshape(1, 8 * rows)
    shape = (2, highs, bins)
    flip, ahead, o_b = [lax.broadcasted_iota(jnp.int32, shape, i) for i in range(3)]
    o_y = jnp.where(flip == 0, 1 - y, y)
    wanted = index_of((high + ahead) % highs, low, o_y, x, core) * bins + o_b
    mix = jnp.where(wanted.reshape(2 * highs * bins, 1) == chip_t, chip_w, 0.0).astype(jnp.bfloat16)

    all_w = info[..., 0, :].reshape(1, n * rows)
    all_t = info[..., 2, :].astype(jnp.int32).reshape(1, n * rows)
    own = me * bins + lax.broadcasted_iota(jnp.int32, (bins, 1), 0)
    totals = jnp.sum(jnp.where(own == all_t, all_w, 0.0), axis=1)
    least = jnp.broadcast_to(jnp.maximum(totals, 1.0)[:, None], (bins, 128))
    means = sum_blocks(n, rot_count, mix, least, parts, sibs)
    return means.transpose(1, 0, 2), weights


def solution(mesh):
    return jax.shard_map(
        body,
        mesh=mesh,
        in_specs=(P("tmpl", "dom"), P("tmpl", None, "dom"), P("tmpl", None), P("tmpl")),
        out_specs=(P("tmpl", None, "dom"), P("tmpl")),
        check_vma=False,
    )
```
